256 devices in a mesh: gx: 8 (over y_lo, x), gy: 16 (over y_hi, z), gz: 2 (over core).
Axes of the slice: x: 4, y: 4 (y_hi: 2, y_lo: 2; y = y_hi * 2 + y_lo), z: 8, core: 2. Of those that a mesh axis runs over, the one named last changes fastest.
Arguments:
- surface_ids: int32 [256, 256, 256], P('gx', 'gy', 'gz'), may hold values from 0 to 256, as said below
- class_map: int32 [256, 256, 256], P('gx', 'gy', 'gz'), may hold values from 0 to 3
- conductivity: float32 [256, 256, 256], P('gx', 'gy', 'gz'), may hold values from 0.5 to 2
- normals: float32 [3, 256], replicated, may hold values from -9 to 9
- class_table: float32 [4], replicated, may hold values from 0.25 to 1
Outputs:
- distance: float32 [256, 256, 256], P('gx', 'gy', 'gz')
The draws below stay inside these ranges and needn't reach their ends.
Inputs may be any that keep to these rules, and one draw needn't show every extreme that they name: `surface_ids`: 0 marks a cell without a source and k a cell of patch k; each cell holds a source with probability one quarter, of a patch drawn evenly.
All inputs are finite; a program needn't handle non-finite values.
Results may differ from the reference program's by a relative error of at most 0.0003.
Values sent between devices are 32-bit elements; how exact they have to be, the bound alone decides.
A program may use at most 128 MiB of HBM per device.

```python
import math
import jax
import jax.numpy as jnp
from jax import lax

N = 256
STEPS = 8
K = 256
CLASSES = 4


def draw_surface_ids(key, part):
    first_key, second_key = jax.random.split(jax.random.fold_in(key, 11))
    patch_ids = jax.random.randint(first_key, (N, N, N), 1, K + 1)
    keeping = jax.random.randint(second_key, (N, N, N), 0, 4) == 0
    return jnp.where(keeping, patch_ids, 0).astype(jnp.int32)


def touch_ends(array, rng, smallest, largest):
    dims = array.shape
    index_at = [jax.random.randint(jax.random.fold_in(rng, axis), (), 0, dims[axis]) for axis in range(len(dims))]
    array = array.at[tuple(index_at)].set(smallest)
    longest = dims.index(max(dims))
    index_at[longest] = (index_at[longest] + 1) % dims[longest]
    return array.at[tuple(index_at)].set(largest)


def levels(stream_key, shape, cuts, low, largest):
    gain, own = 1.0, jax.random.fold_in(stream_key, 6)
    for position, blocks in cuts:
        steps = jnp.exp(jax.random.uniform(jax.random.fold_in(own, position), (blocks,), jnp.float32, low / len(cuts), largest / len(cuts)))
        gain = gain * jnp.repeat(steps, shape[position] // blocks).reshape([-1 if axis == position else 1 for axis in range(len(shape))])
    return gain


def gaussian(key, shape, spread, limit, kind=jnp.bfloat16):
    return jnp.clip(spread * jax.random.normal(key, shape, jnp.float32), -limit, limit).astype(kind)


def setup_inputs(seed: int = 0) -> dict:
    splits = jax.random.split(jax.random.key(seed), 6)
    surface_ids = draw_surface_ids(jax.random.fold_in(splits[5], 71), 0)
    class_map = touch_ends(jax.random.randint(splits[1], (N, N, N), 0, CLASSES), jax.random.fold_in(splits[1], 1), 0, CLASSES - 1).astype(jnp.int32)
    conductivity = jnp.clip(jnp.exp(math.log(2.0) - 1.3862944 * jax.random.uniform(splits[2], (N, N, N), jnp.float32) ** levels(splits[2], (N, N, N), ((0, 8), (1, 16), (2, 2)), -0.2, 0.2)), 0.5, 2.0)
    normals = gaussian(splits[3], (3, K), 1.5, 9.0, jnp.float32)
    class_table = jnp.clip(jnp.exp(jax.random.uniform(splits[4], (CLASSES,), jnp.float32, math.log(0.25), math.log(1.0))), 0.25, 1.0)
    return {"surface_ids": surface_ids, "class_map": class_map, "conductivity": conductivity, "normals": normals, "class_table": class_table}


time_step = 0.08
norm_floor = 0.5
offsets = ((1, 0, 0), (-1, 0, 0), (0, 1, 0), (0, -1, 0), (0, 0, 1), (0, 0, -1))

def shifted(padded, offset):
    extent = padded.shape[-3:]
    return padded[..., 1 + offset[0]:extent[0] - 1 + offset[0], 1 + offset[1]:extent[1] - 1 + offset[1], 1 + offset[2]:extent[2] - 1 + offset[2]]

def diffuse(padded, root_field):
    center = shifted(padded, (0, 0, 0))
    middle = shifted(root_field, (0, 0, 0))
    inflow = jnp.zeros_like(center)
    for offset in offsets:
        inflow = inflow + shifted(root_field, offset) * (shifted(padded, offset) - center)
    return center + time_step * middle * inflow

def cosine_table(length):
    wave_number = jnp.arange(length, dtype=jnp.float32)[:, None]
    sample = jnp.arange(length, dtype=jnp.float32)[None, :]
    factor = jnp.where(wave_number == 0, jnp.sqrt(1.0 / length), jnp.sqrt(2.0 / length))
    return factor * jnp.cos(jnp.pi * wave_number * (2.0 * sample + 1.0) / (2.0 * length))

def eigen_values(length):
    wave_number = jnp.arange(length, dtype=jnp.float32)
    return 2.0 - 2.0 * jnp.cos(jnp.pi * wave_number / length)

def normalize(heat_field):
    magnitude = jnp.sqrt(heat_field[0] * heat_field[0] + heat_field[1] * heat_field[1] + heat_field[2] * heat_field[2])
    return heat_field / jnp.maximum(magnitude, norm_floor)

def reference(surface_ids, class_map, conductivity, normals, class_table):
    lookup_table = jnp.concatenate([jnp.zeros((3, 1), jnp.float32), normals], axis=1)
    source = jnp.take(lookup_table, surface_ids, axis=1)
    conduct = class_table[class_map] * conductivity
    padded_root = jnp.pad(jnp.sqrt(conduct), 1)

    def evolve(component):
        for step_index in range(STEPS):
            component = diffuse(jnp.pad(component, 1), padded_root)
        return component
    heat_field = lax.map(evolve, source)
    unit_field = normalize(heat_field)
    faces_x = jnp.pad(unit_field[0], ((1, 1), (0, 0), (0, 0)))
    faces_y = jnp.pad(unit_field[1], ((0, 0), (1, 1), (0, 0)))
    faces_z = jnp.pad(unit_field[2], ((0, 0), (0, 0), (1, 1)))
    part_x = 0.5 * (faces_x[2:] - faces_x[:-2])
    part_y = 0.5 * (faces_y[:, 2:] - faces_y[:, :-2])
    part_z = 0.5 * (faces_z[:, :, 2:] - faces_z[:, :, :-2])
    divergence = part_x + part_y + part_z
    cosine = cosine_table(N)
    highest = lax.Precision.HIGHEST
    spectrum = jnp.einsum('kn,nyz->kyz', cosine, divergence, precision=highest)
    spectrum = jnp.einsum('kn,xnz->xkz', cosine, spectrum, precision=highest)
    spectrum = jnp.einsum('kn,xyn->xyk', cosine, spectrum, precision=highest)
    spectra = eigen_values(N)
    screen = 4.0 / (N * N)
    divisor = spectra[:, None, None] + spectra[None, :, None] + spectra[None, None, :] + screen
    solved = -spectrum / divisor
    solved = jnp.einsum('kn,kyz->nyz', cosine, solved, precision=highest)
    solved = jnp.einsum('kn,xkz->xnz', cosine, solved, precision=highest)
    distance = jnp.einsum('kn,xyk->xyn', cosine, solved, precision=highest)
    return distance
```

```python
import jax
import jax.numpy as jnp
import numpy as np
from jax import lax
from jax.experimental import pallas as pl
from jax.experimental.pallas import tpu as pltpu
from jax.sharding import PartitionSpec as P

N = 256
STEPS = 8
CLASSES = 4
HALO = STEPS + 1
XE = 16 + 2 * HALO
YE = 32
time_step = 0.08
norm_floor = 0.5
f32 = jnp.float32
bf16 = jnp.bfloat16
MESH = pl.DeviceIdType.MESH


def cosine_table():
    wave_number = np.arange(N, dtype=np.float32)[:, None]
    sample = np.arange(N, dtype=np.float32)[None, :]
    factor = np.where(wave_number == 0, np.sqrt(np.float32(1.0 / N)), np.sqrt(np.float32(2.0 / N)))
    angle = np.float32(np.pi) * wave_number * (np.float32(2.0) * sample + np.float32(1.0)) / np.float32(2.0 * N)
    return (factor * np.cos(angle)).astype(np.float32)


def eigen_values():
    wave_number = np.arange(N, dtype=np.float32)
    return (np.float32(2.0) - np.float32(2.0) * np.cos(np.float32(np.pi) * wave_number / np.float32(N))).astype(np.float32)


def halves(table):
    high = table.astype(jnp.bfloat16)
    low = (table - high.astype(np.float32)).astype(jnp.bfloat16)
    return np.stack([high, low])


def split(values):
    high = values.astype(bf16)
    return high, (values - high.astype(f32)).astype(bf16)


def product(left, right):
    dot = lambda a, b: jnp.dot(a, b, preferred_element_type=f32)
    return dot(left[0], right[0]) + (dot(left[1], right[0]) + dot(left[0], right[1]))


def swap8(tile):
    row = lax.broadcasted_iota(jnp.int32, (8, 128), 0)
    group = lax.broadcasted_iota(jnp.int32, (8, 128), 1) // 16
    for bit in (1, 2, 4):
        row_bit = (row // bit) % 2
        group_bit = (group // bit) % 2
        if bit == 4:
            other = pltpu.roll(pltpu.roll(tile, 4, 0), 64, 1)
        else:
            forth = pltpu.roll(pltpu.roll(tile, bit, 0), 128 - 16 * bit, 1)
            back = pltpu.roll(pltpu.roll(tile, 8 - bit, 0), 16 * bit, 1)
            other = jnp.where(row_bit == 1, forth, back)
        tile = jnp.where(row_bit == group_bit, tile, other)
    return tile


def halo_copies(field, rows, ext, row_ext, send_sem, recv_sem):
    gx, gy, gz = lax.axis_index("gx"), lax.axis_index("gy"), lax.axis_index("gz")
    lanes = pl.ds(pl.multiple_of(gz * 128, 128), 128)
    copies = []
    for dy in (1, -1, 0):
        src_rows = {1: pl.ds(8, 8), -1: pl.ds(0, 8), 0: pl.ds(0, 16)}[dy]
        dst_rows = {1: pl.ds(0, 8), -1: pl.ds(24, 8), 0: pl.ds(8, 16)}[dy]
        to_y = lax.rem(gy + dy + 16, 16)
        for other in (0, 1):
            core = 1 - gz if other else gz
            to_x = lax.rem(gx + 1 - 2 * core + 8, 8)
            parts = [
                (field.at[:, pl.ds(7 * core, 25), src_rows, :], ext.at[:, pl.ds(9 * (1 - core), 25), dst_rows, lanes], gx),
                (field.at[:, pl.ds(23 * (1 - core), 9), src_rows, :], ext.at[:, pl.ds(25 * core, 9), dst_rows, lanes], to_x),
            ]
            if dy:
                side = 0 if dy == 1 else 1
                parts += [
                    (rows.at[side], row_ext.at[side, :, pl.ds(16, 32), lanes], gx),
                    (rows.at[side, :, pl.ds(pl.multiple_of(16 * (1 - core), 16), 16), :],
                     row_ext.at[side, :, pl.ds(pl.multiple_of(48 * core, 16), 16), lanes], to_x),
                ]
            for index, (src, dst, x) in enumerate(parts):
                slot = len(copies)
                if dy == 0 and other == 0 and index == 0:
                    copies.append(pltpu.make_async_copy(src, dst, recv_sem.at[slot]))
                else:
                    copies.append(pltpu.make_async_remote_copy(
                        src, dst, send_sem.at[slot], recv_sem.at[slot],
                        device_id=(x, to_y, core), device_id_type=MESH))
    return copies


def greet_halo(barrier):
    gx, gy, gz = lax.axis_index("gx"), lax.axis_index("gy"), lax.axis_index("gz")
    from_x = lax.rem(gx + 2 * gz - 1 + 8, 8)
    count = 0
    for dy in (1, -1, 0):
        y = lax.rem(gy + dy + 16, 16)
        for core in (0, 1):
            pl.semaphore_signal(barrier, inc=1, device_id=(from_x, y, core), device_id_type=MESH)
            count += 1
        pl.semaphore_signal(barrier, inc=1, device_id=(gx, y, 1 - gz), device_id_type=MESH)
        count += 1
        if dy:
            pl.semaphore_signal(barrier, inc=1, device_id=(gx, y, gz), device_id_type=MESH)
            count += 1
    return count


def fill_field(ids_ref, class_ref, cond_ref, table_ref, field, rows):
    def plane(i, _):
        classes = class_ref[i]
        value = jnp.full(classes.shape, table_ref[0], f32)
        for k in range(1, CLASSES):
            value = jnp.where(classes == k, table_ref[k], value)
        field[0, i] = jnp.sqrt(value * cond_ref[i])
        field[1, i] = ids_ref[i].astype(f32)
        return 0
    lax.fori_loop(0, 32, plane, 0)
    for which in range(2):
        rows[0, which] = field[which, :, 7, :]
        rows[1, which] = field[which, :, 8, :]


def lookup(ids_float, tables):
    index = ids_float.astype(jnp.int32) - 1
    low = jnp.bitwise_and(index, 127)
    found = []
    for first, second in tables:
        a = jnp.take_along_axis(first, low, axis=1)
        b = jnp.take_along_axis(second, low, axis=1)
        found.append(jnp.where(index < 0, 0.0, jnp.where(index < 128, a, b)))
    return found


def z_sides(values):
    lane = lax.broadcasted_iota(jnp.int32, (values.shape[0], 128), 1)
    low, high = values[:, :128], values[:, 128:]
    low_up, high_up = pltpu.roll(low, 1, 1), pltpu.roll(high, 1, 1)
    low_down, high_down = pltpu.roll(low, 127, 1), pltpu.roll(high, 127, 1)
    before = (jnp.where(lane == 0, 0.0, low_up), jnp.where(lane == 0, low_up, high_up))
    after = (jnp.where(lane == 127, high_down, low_down), jnp.where(lane == 127, 0.0, high_down))
    return before, after


def heat_part(normals_ref, ext, row_ext, forward_ref, out_ref, root, gain, keep, wa, wb, row_root, row_w, div, mixed):
    gx, gy, gz = lax.axis_index("gx"), lax.axis_index("gy"), lax.axis_index("gz")
    x0 = gx * 32 + gz * 16
    y0 = gy * 16

    def tables(r):
        return [tuple(jnp.broadcast_to(normals_ref[j:j + 1, h * 128:(h + 1) * 128], (r, 128)) for h in range(2)) for j in range(3)]

    y_of = lax.broadcasted_iota(jnp.int32, (YE, 256), 0) + (y0 - 8)
    y_inside = jnp.logical_and(y_of >= 0, y_of < N)

    def start(i, _):
        x = x0 - HALO + i
        inside = jnp.logical_and(y_inside, jnp.logical_and(x >= 0, x < N))
        value = jnp.where(inside, ext[0, i], 0.0)
        root[i] = value
        for h in range(2):
            lanes = pl.ds(h * 128, 128)
            found = lookup(ext[1, i, :, lanes], tables(YE))
            for j in range(3):
                wa[j, i, :, lanes] = found[j] * value[:, h * 128:(h + 1) * 128]
        return 0
    lax.fori_loop(0, XE, start, 0)

    x_of = lax.broadcasted_iota(jnp.int32, (64, 256), 0) + (gx * 32 - 16)
    x_inside = jnp.logical_and(x_of >= 0, x_of < N)
    for side in range(2):
        y = y0 - 9 if side == 0 else y0 + 24
        inside = jnp.logical_and(x_inside, jnp.logical_and(y >= 0, y < N))
        value = jnp.where(inside, row_ext[side, 0], 0.0)
        row_root[side] = value
        for h in range(2):
            lanes = pl.ds(h * 128, 128)
            found = lookup(row_ext[side, 1, :, lanes], tables(64))
            for j in range(3):
                row_w[side, j, :, lanes] = found[j] * value[:, h * 128:(h + 1) * 128]

    y_index = lax.broadcasted_iota(jnp.int32, (YE, 256), 0)

    def around(values, before_row=None, after_row=None):
        up, down = pltpu.roll(values, 1, 0), pltpu.roll(values, YE - 1, 0)
        if before_row is not None:
            up = jnp.where(y_index == 0, before_row, up)
            down = jnp.where(y_index == YE - 1, after_row, down)
        before, after = z_sides(values)
        side = jnp.concatenate([before[0] + after[0], before[1] + after[1]], axis=1)
        return (up + down) + side

    def coefficients(i, _):
        r = i + 7 + 16 * gz
        center = root[i]
        total = around(center, row_root[0, pl.ds(r, 1), :], row_root[1, pl.ds(r, 1), :]) + (root[i - 1] + root[i + 1])
        keep[i] = 1.0 - time_step * center * total
        gain[i] = time_step * center * center
        return 0
    lax.fori_loop(1, XE - 1, coefficients, 0)

    for step in range(1, STEPS + 1):
        src, dst = (wa, wb) if step % 2 else (wb, wa)

        def plane(i, _, src=src, dst=dst, step=step):
            a, d = keep[i], gain[i]
            r = i + 7 + 16 * gz
            for j in range(3):
                center = src[j, i]
                if step == 1:
                    total = around(center, row_w[0, j, pl.ds(r, 1), :], row_w[1, j, pl.ds(r, 1), :])
                else:
                    total = around(center)
                total = total + (src[j, i - 1] + src[j, i + 1])
                dst[j, i] = a * center + d * total
            return 0
        lax.fori_loop(step, XE - step, plane, 0)

    def unit(i, _):
        w = [wa[j, i] for j in range(3)]
        size = jnp.sqrt(w[0] * w[0] + w[1] * w[1] + w[2] * w[2])
        floor = jnp.maximum(jnp.maximum(size, norm_floor * root[i]), 1e-30)
        scale = 0.5 / floor
        for j in range(3):
            wb[j, i] = w[j] * scale
        return 0
    lax.fori_loop(STEPS, XE - STEPS, unit, 0)

    def divergence(k, _):
        i = k + HALO
        u1 = wb[1, i]
        before, after = z_sides(wb[2, i])
        part_z = jnp.concatenate([after[0] - before[0], after[1] - before[1]], axis=1)
        value = (wb[0, i + 1] - wb[0, i - 1]) + (pltpu.roll(u1, YE - 1, 0) - pltpu.roll(u1, 1, 0)) + part_z
        for h in range(2):
            div[h, pl.ds(pl.multiple_of(k * 16, 16), 16), :] = value[8:24, h * 128:(h + 1) * 128]
        return 0
    lax.fori_loop(0, 16, divergence, 0)

    lines = jnp.concatenate(
        [jnp.concatenate([div[h, pl.ds(y, 16, stride=16), :] for y in range(16)], axis=0) for h in range(2)], axis=1)
    mixed[...] = product(split(lines), (forward_ref[0], forward_ref[1]))

    def spread(y, _):
        for xh in range(2):
            for ah in range(2):
                tile = mixed[pl.ds(pl.multiple_of(y * 16 + xh * 8, 8), 8), pl.ds(ah * 128, 128)]
                out_ref[xh, pl.ds(ah * 128 + y, 8, stride=16), :] = swap8(tile)
        return 0
    lax.fori_loop(0, 16, spread, 0)


def y_group(index):
    return (lax.axis_index("gx"), index, lax.axis_index("gz"))


def x_group(index):
    return (index // 2, lax.axis_index("gy"), index % 2)


def exchange(src, dst, me, where, send_sem, recv_sem):
    def copy(d):
        to = lax.rem(me + d, 16)
        return pltpu.make_async_remote_copy(
            src.at[:, pl.ds(pl.multiple_of(to * 16, 16), 16), :],
            dst.at[:, pl.ds(pl.multiple_of(me * 16, 16), 16), :],
            send_sem.at[d], recv_sem.at[d], device_id=where(to), device_id_type=MESH)

    def start(d, _):
        copy(d).start()
        return 0
    lax.fori_loop(1, 16, start, 0)
    own = pl.ds(pl.multiple_of(me * 16, 16), 16)
    dst[:, own, :] = src[:, own, :]

    def wait(d, _):
        copy(d).wait()
        return 0
    lax.fori_loop(1, 16, wait, 0)


def whole(ref):
    return jnp.concatenate([ref[0], ref[1]], axis=1)


def turn(values, mixed, dst):
    mixed[...] = values

    def block(b, _):
        for rh in range(2):
            for gh in range(2):
                tile = mixed[pl.ds(pl.multiple_of(b * 16 + rh * 8, 8), 8), pl.ds(gh * 128, 128)]
                dst[rh, pl.ds(pl.multiple_of(b * 16 + gh * 8, 8), 8), :] = swap8(tile)
        return 0
    lax.fori_loop(0, 16, block, 0)


def greet_groups(barrier):
    gx, gy, gz = lax.axis_index("gx"), lax.axis_index("gy"), lax.axis_index("gz")
    group = gx * 2 + gz

    def greet(d, _):
        pl.semaphore_signal(barrier, inc=1, device_id=y_group(lax.rem(gy + d, 16)), device_id_type=MESH)
        pl.semaphore_signal(barrier, inc=1, device_id=x_group(lax.rem(group + d, 16)), device_id_type=MESH)
        return 0
    lax.fori_loop(1, 16, greet, 0)
    return 30


def solve_part(s1, forward_ref, cosine_ref, eigen_x, eigen_y, eigen_z, out_ref, r2, s2, r3, s3, r4, s4, r5, lines, own_out, peer_out, mixed,
               send_sem, recv_sem, last_send, last_recv):
    gx, gy, gz = lax.axis_index("gx"), lax.axis_index("gy"), lax.axis_index("gz")
    group = gx * 2 + gz
    cosine = (cosine_ref[0], cosine_ref[1])
    forward = (forward_ref[0], forward_ref[1])
    exchange(s1, r2, gy, y_group, send_sem.at[0], recv_sem.at[0])
    turn(product(cosine, split(whole(r2))), mixed, s2)
    exchange(s2, r3, group, x_group, send_sem.at[1], recv_sem.at[1])
    spectrum = product(cosine, split(whole(r3)))
    rest = eigen_y[pl.ds(group, 1), :] + eigen_z[pl.ds(gy, 1), :]
    eigen = jnp.concatenate([eigen_x[...], eigen_x[...]], axis=1)
    solved = -spectrum / (eigen + rest + 4.0 / (N * N))
    turn(product(forward, split(solved)), mixed, s3)
    exchange(s3, r4, group, x_group, send_sem.at[2], recv_sem.at[2])
    values = product(forward, split(whole(r4)))
    for h in range(2):
        s4[h] = values[:, h * 128:(h + 1) * 128]
    exchange(s4, r5, gy, y_group, send_sem.at[3], recv_sem.at[3])

    def gather(y, _):
        for xh in range(2):
            for ah in range(2):
                tile = r5[xh, pl.ds(ah * 128 + y, 8, stride=16), :]
                lines[pl.ds(pl.multiple_of(y * 16 + xh * 8, 8), 8), pl.ds(ah * 128, 128)] = swap8(tile)
        return 0
    lax.fori_loop(0, 16, gather, 0)
    values = product(split(lines[...]), cosine)
    first = gz == 0
    mine = jnp.where(first, values[:, :128], values[:, 128:])
    theirs = jnp.where(first, values[:, 128:], values[:, :128])
    for y in range(16):
        peer_out[pl.ds(y, 16, stride=16), :] = theirs[y * 16:(y + 1) * 16]
    rows = pl.ds(pl.multiple_of(gz * 256, 256), 256)
    copy = pltpu.make_async_remote_copy(
        peer_out, out_ref.at[rows, :], last_send, last_recv, device_id=(gx, gy, 1 - gz), device_id_type=MESH)
    copy.start()
    for y in range(16):
        own_out[pl.ds(y, 16, stride=16), :] = mine[y * 16:(y + 1) * 16]
    out_ref[rows, :] = own_out[...]
    copy.wait()


VM = pl.BlockSpec(memory_space=pltpu.VMEM)
SM = pl.BlockSpec(memory_space=pltpu.SMEM)
DMA = pltpu.SemaphoreType.DMA
LIMIT = 48 * 1024 * 1024


def vmem(*shape):
    return pltpu.VMEM(shape, f32)


def first_kernel(ids_ref, class_ref, cond_ref, table_ref, ext, row_ext, field, rows, send_sem, recv_sem):
    barrier = pltpu.get_barrier_semaphore()
    count = greet_halo(barrier)
    fill_field(ids_ref, class_ref, cond_ref, table_ref, field, rows)
    pl.semaphore_wait(barrier, count)
    copies = halo_copies(field, rows, ext, row_ext, send_sem, recv_sem)
    for copy in copies:
        copy.start()
    for copy in copies:
        copy.wait()


def third_kernel(s1, *rest):
    barrier = pltpu.get_barrier_semaphore()
    count = greet_groups(barrier)
    pl.semaphore_wait(barrier, count)
    solve_part(s1, *rest)


def per_device(surface_ids, class_map, conductivity, normals, class_table):
    cosine = cosine_table()
    eigen = eigen_values()
    cosine_pair, forward_pair = jnp.asarray(halves(cosine)), jnp.asarray(halves(cosine.T.copy()))
    eigen_x = jnp.asarray(np.repeat(eigen[:, None], 128, axis=1))
    eigen_y = jnp.asarray(np.repeat(eigen.reshape(16, 16), 16, axis=1))
    eigen_z = jnp.asarray(np.tile(eigen.reshape(16, 16), (1, 16)))
    ext, row_ext = pl.pallas_call(
        first_kernel,
        out_shape=(jax.ShapeDtypeStruct((2, XE, YE, 256), f32), jax.ShapeDtypeStruct((2, 2, 64, 256), f32)),
        in_specs=[VM, VM, VM, SM], out_specs=(VM, VM),
        scratch_shapes=[vmem(2, 32, 16, 128), vmem(2, 2, 32, 128), DMA((20,)), DMA((20,))],
        compiler_params=pltpu.CompilerParams(collective_id=0, has_side_effects=True, vmem_limit_bytes=LIMIT),
    )(surface_ids, class_map, conductivity, class_table)
    s1 = pl.pallas_call(
        heat_part,
        out_shape=jax.ShapeDtypeStruct((2, 256, 128), f32),
        in_specs=[VM, VM, VM, VM], out_specs=VM,
        scratch_shapes=[vmem(XE, YE, 256), vmem(XE, YE, 256), vmem(XE, YE, 256), vmem(3, XE, YE, 256), vmem(3, XE, YE, 256),
                        vmem(2, 64, 256), vmem(2, 3, 64, 256), vmem(2, 256, 128), vmem(256, 256)],
        compiler_params=pltpu.CompilerParams(vmem_limit_bytes=LIMIT),
    )(normals, ext, row_ext, forward_pair)
    out = pl.pallas_call(
        third_kernel,
        out_shape=jax.ShapeDtypeStruct((512, 128), f32),
        in_specs=[VM] * 6, out_specs=VM,
        scratch_shapes=[vmem(2, 256, 128) for _ in range(7)] + [vmem(256, 256), vmem(256, 128), vmem(256, 128), vmem(256, 256),
                        DMA((4, 16)), DMA((4, 16)), DMA(()), DMA(())],
        compiler_params=pltpu.CompilerParams(collective_id=1, has_side_effects=True, vmem_limit_bytes=LIMIT),
    )(s1, forward_pair, cosine_pair, eigen_x, eigen_y, eigen_z)
    return out.reshape(32, 16, 128)


def solution(mesh):
    spec = P("gx", "gy", "gz")
    return jax.shard_map(
        per_device, mesh=mesh, in_specs=(spec, spec, spec, P(), P()), out_specs=spec, check_vma=False
    )
```

```python
import jax
import jax.numpy as jnp
import numpy as np
from jax import lax
from jax.experimental import pallas as pl
from jax.experimental.pallas import tpu as pltpu
from jax.sharding import PartitionSpec as P

N = 256
STEPS = 8
CLASSES = 4
HALO = STEPS + 1
XE = 16 + 2 * HALO
YE = 32
time_step = 0.08
norm_floor = 0.5
f32 = jnp.float32
bf16 = jnp.bfloat16
MESH = pl.DeviceIdType.MESH


def cosine_table():
    wave_number = np.arange(N, dtype=np.float32)[:, None]
    sample = np.arange(N, dtype=np.float32)[None, :]
    factor = np.where(wave_number == 0, np.sqrt(np.float32(1.0 / N)), np.sqrt(np.float32(2.0 / N)))
    angle = np.float32(np.pi) * wave_number * (np.float32(2.0) * sample + np.float32(1.0)) / np.float32(2.0 * N)
    return (factor * np.cos(angle)).astype(np.float32)


def eigen_values():
    wave_number = np.arange(N, dtype=np.float32)
    return (np.float32(2.0) - np.float32(2.0) * np.cos(np.float32(np.pi) * wave_number / np.float32(N))).astype(np.float32)


def halves(table):
    high = table.astype(jnp.bfloat16)
    low = (table - high.astype(np.float32)).astype(jnp.bfloat16)
    return np.stack([high, low])


def split(values):
    high = values.astype(bf16)
    return high, (values - high.astype(f32)).astype(bf16)


def product(left, right):
    dot = lambda a, b: jnp.dot(a, b, preferred_element_type=f32)
    return dot(left[0], right[0]) + (dot(left[1], right[0]) + dot(left[0], right[1]))


def swap8(tile):
    row = lax.broadcasted_iota(jnp.int32, (8, 128), 0)
    group = lax.broadcasted_iota(jnp.int32, (8, 128), 1) // 16
    for bit in (1, 2, 4):
        row_bit = (row // bit) % 2
        group_bit = (group // bit) % 2
        if bit == 4:
            other = pltpu.roll(pltpu.roll(tile, 4, 0), 64, 1)
        else:
            forth = pltpu.roll(pltpu.roll(tile, bit, 0), 128 - 16 * bit, 1)
            back = pltpu.roll(pltpu.roll(tile, 8 - bit, 0), 16 * bit, 1)
            other = jnp.where(row_bit == 1, forth, back)
        tile = jnp.where(row_bit == group_bit, tile, other)
    return tile


def halo_copies(field, rows, ext, row_ext, send_sem, recv_sem):
    gx, gy, gz = lax.axis_index("gx"), lax.axis_index("gy"), lax.axis_index("gz")
    lanes = pl.ds(pl.multiple_of(gz * 128, 128), 128)
    copies = []
    for dy in (1, -1, 0):
        src_rows = {1: pl.ds(8, 8), -1: pl.ds(0, 8), 0: pl.ds(0, 16)}[dy]
        dst_rows = {1: pl.ds(0, 8), -1: pl.ds(24, 8), 0: pl.ds(8, 16)}[dy]
        to_y = lax.rem(gy + dy + 16, 16)
        for other in (0, 1):
            core = 1 - gz if other else gz
            to_x = lax.rem(gx + 1 - 2 * core + 8, 8)
            parts = [
                (field.at[:, pl.ds(7 * core, 25), src_rows, :], ext.at[:, pl.ds(9 * (1 - core), 25), dst_rows, lanes], gx),
                (field.at[:, pl.ds(23 * (1 - core), 9), src_rows, :], ext.at[:, pl.ds(25 * core, 9), dst_rows, lanes], to_x),
            ]
            if dy:
                side = 0 if dy == 1 else 1
                parts += [
                    (rows.at[side], row_ext.at[side, :, pl.ds(16, 32), lanes], gx),
                    (rows.at[side, :, pl.ds(pl.multiple_of(16 * (1 - core), 16), 16), :],
                     row_ext.at[side, :, pl.ds(pl.multiple_of(48 * core, 16), 16), lanes], to_x),
                ]
            for index, (src, dst, x) in enumerate(parts):
                slot = len(copies)
                if dy == 0 and other == 0 and index == 0:
                    copies.append(pltpu.make_async_copy(src, dst, recv_sem.at[slot]))
                else:
                    copies.append(pltpu.make_async_remote_copy(
                        src, dst, send_sem.at[slot], recv_sem.at[slot],
                        device_id=(x, to_y, core), device_id_type=MESH))
    return copies


def greet_halo(barrier):
    gx, gy, gz = lax.axis_index("gx"), lax.axis_index("gy"), lax.axis_index("gz")
    from_x = lax.rem(gx + 2 * gz - 1 + 8, 8)
    count = 0
    for dy in (1, -1, 0):
        y = lax.rem(gy + dy + 16, 16)
        for core in (0, 1):
            pl.semaphore_signal(barrier, inc=1, device_id=(from_x, y, core), device_id_type=MESH)
            count += 1
        pl.semaphore_signal(barrier, inc=1, device_id=(gx, y, 1 - gz), device_id_type=MESH)
        count += 1
        if dy:
            pl.semaphore_signal(barrier, inc=1, device_id=(gx, y, gz), device_id_type=MESH)
            count += 1
    return count


def fill_field(ids_ref, class_ref, cond_ref, table_ref, field, rows):
    def plane(i, _):
        classes = class_ref[i]
        value = jnp.full(classes.shape, table_ref[0], f32)
        for k in range(1, CLASSES):
            value = jnp.where(classes == k, table_ref[k], value)
        field[0, i] = jnp.sqrt(value * cond_ref[i])
        field[1, i] = ids_ref[i].astype(f32)
        return 0
    lax.fori_loop(0, 32, plane, 0)
    for which in range(2):
        rows[0, which] = field[which, :, 7, :]
        rows[1, which] = field[which, :, 8, :]


def lookup(ids_float, tables):
    index = ids_float.astype(jnp.int32) - 1
    low = jnp.bitwise_and(index, 127)
    found = []
    for first, second in tables:
        a = jnp.take_along_axis(first, low, axis=1)
        b = jnp.take_along_axis(second, low, axis=1)
        found.append(jnp.where(index < 0, 0.0, jnp.where(index < 128, a, b)))
    return found


SWAP_UNROLL = 16
UNROLL = 6
UNALIGNED = True
LOOKUP_UNROLL = 4


def z_sum(low, high):
    lane = lax.broadcasted_iota(jnp.int32, low.shape, 1)
    low_up, high_up = pltpu.roll(low, 1, 1), pltpu.roll(high, 1, 1)
    low_down, high_down = pltpu.roll(low, 127, 1), pltpu.roll(high, 127, 1)
    first, last = lane == 0, lane == 127
    return (jnp.where(first, 0.0, low_up) + jnp.where(last, high_down, low_down),
            jnp.where(first, low_up, high_up) + jnp.where(last, 0.0, high_down))


def z_difference(low, high):
    lane = lax.broadcasted_iota(jnp.int32, low.shape, 1)
    low_up, high_up = pltpu.roll(low, 1, 1), pltpu.roll(high, 1, 1)
    low_down, high_down = pltpu.roll(low, 127, 1), pltpu.roll(high, 127, 1)
    first, last = lane == 0, lane == 127
    return (jnp.where(last, high_down, low_down) - jnp.where(first, 0.0, low_up),
            jnp.where(last, 0.0, high_down) - jnp.where(first, low_up, high_up))


BODY = pl.ds(8, YE)


def neighbours(ref, lead, i):
    center = [ref[lead + (h, i, BODY)] for h in range(2)]
    sides = z_sum(*center)
    total = []
    for h in range(2):
        if UNALIGNED:
            y = ref[lead + (h, i, pl.ds(7, YE))] + ref[lead + (h, i, pl.ds(9, YE))]
        else:
            y = pltpu.roll(center[h], 1, 0) + pltpu.roll(center[h], YE - 1, 0)
        x = ref[lead + (h, i - 1, BODY)] + ref[lead + (h, i + 1, BODY)]
        total.append((x + y) + sides[h])
    return center, total


def heat_part(normals_ref, ext, row_ext, forward_ref, out_ref, root, gain, keep, wa, wb, div, mixed):
    gx, gy, gz = lax.axis_index("gx"), lax.axis_index("gy"), lax.axis_index("gz")
    x0 = gx * 32 + gz * 16
    y0 = gy * 16

    def tables(r):
        return [tuple(jnp.broadcast_to(normals_ref[j:j + 1, h * 128:(h + 1) * 128], (r, 128)) for h in range(2)) for j in range(3)]

    y_of = lax.broadcasted_iota(jnp.int32, (YE, 128), 0) + (y0 - 8)
    y_inside = jnp.logical_and(y_of >= 0, y_of < N)

    def start(i, _):
        x = x0 - HALO + i
        x_in = jnp.logical_and(x >= 0, x < N)
        inside = jnp.logical_and(y_inside, x_in)
        r = i + 7 + 16 * gz
        done = []
        for h in range(2):
            lanes = pl.ds(h * 128, 128)
            value = jnp.where(inside, ext[0, i, :, lanes], 0.0)
            found = lookup(ext[1, i, :, lanes], tables(YE))
            done.append((value, [found[j] * value for j in range(3)]))
        for h in range(2):
            root[h, i, BODY] = done[h][0]
            for j in range(3):
                wa[j, h, i, BODY] = done[h][1][j]
        return 0
    lax.fori_loop(0, XE, start, 0, unroll=LOOKUP_UNROLL)

    x_of = lax.broadcasted_iota(jnp.int32, (40, 128), 0) + (x0 - HALO)
    x_inside = jnp.logical_and(x_of >= 0, x_of < N)
    wide = pl.ds(pl.multiple_of(16 * gz, 8), 48)
    for side in range(2):
        y = y0 - 9 if side == 0 else y0 + 24
        inside = jnp.logical_and(x_inside, jnp.logical_and(y >= 0, y < N))
        row = 7 if side == 0 else 40
        for h in range(2):
            lanes = pl.ds(h * 128, 128)
            value = jnp.where(inside, row_ext[side, 0, wide, lanes][7:47], 0.0)
            found = lookup(row_ext[side, 1, wide, lanes][7:47], tables(40))
            root[h, :, row, :] = value[:XE]
            for j in range(3):
                wa[j, h, :, row, :] = (found[j] * value)[:XE]
                wb[j, h, :, row, :] = jnp.zeros((XE, 128), f32)

    def coefficients(i, _):
        center, total = neighbours(root, (), i)
        for h in range(2):
            keep[h, i] = 1.0 - time_step * center[h] * total[h]
            gain[h, i] = time_step * center[h] * center[h]
        return 0
    lax.fori_loop(1, XE - 1, coefficients, 0, unroll=UNROLL)

    for step in range(1, STEPS + 1):
        src, dst = (wa, wb) if step % 2 else (wb, wa)

        def plane(i, _, src=src, dst=dst):
            done = []
            for j in range(3):
                center, total = neighbours(src, (j,), i)
                for h in range(2):
                    done.append((j, h, keep[h, i] * center[h] + gain[h, i] * total[h]))
            for j, h, value in done:
                dst[j, h, i, BODY] = value
            return 0
        lax.fori_loop(step, XE - step, plane, 0, unroll=UNROLL)

    def unit(i, _):
        for h in range(2):
            w = [wa[j, h, i, BODY] for j in range(3)]
            size = jnp.sqrt(w[0] * w[0] + w[1] * w[1] + w[2] * w[2])
            floor = jnp.maximum(jnp.maximum(size, norm_floor * root[h, i, BODY]), 1e-30)
            scale = 0.5 / floor
            for j in range(3):
                wb[j, h, i, BODY] = w[j] * scale
        return 0
    lax.fori_loop(STEPS, XE - STEPS, unit, 0, unroll=UNROLL)

    def divergence(k, _):
        i = k + HALO
        part_z = z_difference(*[wb[2, h, i, pl.ds(16, 16)] for h in range(2)])
        for h in range(2):
            part_x = wb[0, h, i + 1, pl.ds(16, 16)] - wb[0, h, i - 1, pl.ds(16, 16)]
            part_y = wb[1, h, i, pl.ds(17, 16)] - wb[1, h, i, pl.ds(15, 16)]
            div[h, pl.ds(pl.multiple_of(k * 16, 16), 16), :] = part_x + part_y + part_z[h]
        return 0
    lax.fori_loop(0, 16, divergence, 0, unroll=UNROLL)

    lines = jnp.concatenate(
        [jnp.concatenate([div[h, pl.ds(y, 16, stride=16), :] for y in range(16)], axis=0) for h in range(2)], axis=1)
    mixed[...] = product(split(lines), (forward_ref[0], forward_ref[1]))

    def spread(y, _):
        for xh in range(2):
            for ah in range(2):
                tile = mixed[pl.ds(pl.multiple_of(y * 16 + xh * 8, 8), 8), pl.ds(ah * 128, 128)]
                out_ref[xh, pl.ds(ah * 128 + y, 8, stride=16), :] = swap8(tile)
        return 0
    lax.fori_loop(0, 16, spread, 0, unroll=SWAP_UNROLL)


def y_group(index):
    return (lax.axis_index("gx"), index, lax.axis_index("gz"))


def x_group(index):
    return (index // 2, lax.axis_index("gy"), index % 2)


def exchange(src, dst, me, where, send_sem, recv_sem):
    def copy(d):
        to = lax.rem(me + d, 16)
        return pltpu.make_async_remote_copy(
            src.at[:, pl.ds(pl.multiple_of(to * 16, 16), 16), :],
            dst.at[:, pl.ds(pl.multiple_of(me * 16, 16), 16), :],
            send_sem.at[d], recv_sem.at[d], device_id=where(to), device_id_type=MESH)

    def start(d, _):
        copy(d).start()
        return 0
    lax.fori_loop(1, 16, start, 0)
    own = pl.ds(pl.multiple_of(me * 16, 16), 16)
    dst[:, own, :] = src[:, own, :]

    def wait(d, _):
        copy(d).wait()
        return 0
    lax.fori_loop(1, 16, wait, 0)


def whole(ref):
    return jnp.concatenate([ref[0], ref[1]], axis=1)


def turn(values, mixed, dst):
    mixed[...] = values

    def block(b, _):
        for rh in range(2):
            for gh in range(2):
                tile = mixed[pl.ds(pl.multiple_of(b * 16 + rh * 8, 8), 8), pl.ds(gh * 128, 128)]
                dst[rh, pl.ds(pl.multiple_of(b * 16 + gh * 8, 8), 8), :] = swap8(tile)
        return 0
    lax.fori_loop(0, 16, block, 0, unroll=SWAP_UNROLL)


def greet_groups(barrier):
    gx, gy, gz = lax.axis_index("gx"), lax.axis_index("gy"), lax.axis_index("gz")
    group = gx * 2 + gz

    def greet(d, _):
        pl.semaphore_signal(barrier, inc=1, device_id=y_group(lax.rem(gy + d, 16)), device_id_type=MESH)
        pl.semaphore_signal(barrier, inc=1, device_id=x_group(lax.rem(group + d, 16)), device_id_type=MESH)
        return 0
    lax.fori_loop(1, 16, greet, 0)
    return 30


def solve_part(s1, forward_ref, cosine_ref, eigen_x, eigen_y, eigen_z, out_ref, r2, s2, r3, s3, r4, s4, r5, lines, own_out, peer_out, mixed,
               send_sem, recv_sem, last_send, last_recv):
    gx, gy, gz = lax.axis_index("gx"), lax.axis_index("gy"), lax.axis_index("gz")
    group = gx * 2 + gz
    cosine = (cosine_ref[0], cosine_ref[1])
    forward = (forward_ref[0], forward_ref[1])
    exchange(s1, r2, gy, y_group, send_sem.at[0], recv_sem.at[0])
    turn(product(cosine, split(whole(r2))), mixed, s2)
    exchange(s2, r3, group, x_group, send_sem.at[1], recv_sem.at[1])
    spectrum = product(cosine, split(whole(r3)))
    rest = eigen_y[pl.ds(group, 1), :] + eigen_z[pl.ds(gy, 1), :]
    eigen = jnp.concatenate([eigen_x[...], eigen_x[...]], axis=1)
    solved = -spectrum / (eigen + rest + 4.0 / (N * N))
    turn(product(forward, split(solved)), mixed, s3)
    exchange(s3, r4, group, x_group, send_sem.at[2], recv_sem.at[2])
    values = product(forward, split(whole(r4)))
    for h in range(2):
        s4[h] = values[:, h * 128:(h + 1) * 128]
    exchange(s4, r5, gy, y_group, send_sem.at[3], recv_sem.at[3])

    def gather(y, _):
        for xh in range(2):
            for ah in range(2):
                tile = r5[xh, pl.ds(ah * 128 + y, 8, stride=16), :]
                lines[pl.ds(pl.multiple_of(y * 16 + xh * 8, 8), 8), pl.ds(ah * 128, 128)] = swap8(tile)
        return 0
    lax.fori_loop(0, 16, gather, 0, unroll=SWAP_UNROLL)
    values = product(split(lines[...]), cosine)
    first = gz == 0
    mine = jnp.where(first, values[:, :128], values[:, 128:])
    theirs = jnp.where(first, values[:, 128:], values[:, :128])
    for y in range(16):
        peer_out[pl.ds(y, 16, stride=16), :] = theirs[y * 16:(y + 1) * 16]
    rows = pl.ds(pl.multiple_of(gz * 256, 256), 256)
    copy = pltpu.make_async_remote_copy(
        peer_out, out_ref.at[rows, :], last_send, last_recv, device_id=(gx, gy, 1 - gz), device_id_type=MESH)
    copy.start()
    for y in range(16):
        own_out[pl.ds(y, 16, stride=16), :] = mine[y * 16:(y + 1) * 16]
    out_ref[rows, :] = own_out[...]
    copy.wait()


VM = pl.BlockSpec(memory_space=pltpu.VMEM)
SM = pl.BlockSpec(memory_space=pltpu.SMEM)
DMA = pltpu.SemaphoreType.DMA
LIMIT = 48 * 1024 * 1024


def vmem(*shape):
    return pltpu.VMEM(shape, f32)


SCRATCH = dict(
    ids=pltpu.VMEM((32, 16, 128), jnp.int32), classes=pltpu.VMEM((32, 16, 128), jnp.int32), cond=vmem(32, 16, 128),
    forward=pltpu.VMEM((2, 256, 256), bf16), cosine=pltpu.VMEM((2, 256, 256), bf16),
    eigen_x=vmem(256, 128), eigen_y=vmem(16, 256), eigen_z=vmem(16, 256), in_sem=DMA((8,)),
    field=vmem(2, 32, 16, 128), rows=vmem(2, 2, 32, 128), ext=vmem(2, XE, YE, 256), row_ext=vmem(2, 2, 64, 256),
    halo_send=DMA((20,)), halo_recv=DMA((20,)),
    root=vmem(2, XE, 48, 128), gain=vmem(2, XE, YE, 128), keep=vmem(2, XE, YE, 128),
    wa=vmem(3, 2, XE, 48, 128), wb=vmem(3, 2, XE, 48, 128), div=vmem(2, 256, 128), mixed=vmem(256, 256),
    s1=vmem(2, 256, 128), r2=vmem(2, 256, 128), s2=vmem(2, 256, 128), r3=vmem(2, 256, 128), s3=vmem(2, 256, 128),
    r4=vmem(2, 256, 128), s4=vmem(2, 256, 128), r5=vmem(2, 256, 128), lines=vmem(256, 256),
    own_out=vmem(256, 128), peer_out=vmem(256, 128),
    send_sem=DMA((4, 16)), recv_sem=DMA((4, 16)), last_send=DMA(()), last_recv=DMA(()),
)


def whole_kernel(ids_in, class_in, cond_in, forward_in, cosine_in, eigen_x_in, eigen_y_in, eigen_z_in, table_ref, normals_ref, out_ref, *scratch):
    s = dict(zip(SCRATCH, scratch))
    loads = [pltpu.make_async_copy(src, dst, s["in_sem"].at[k]) for k, (src, dst) in enumerate([
        (ids_in, s["ids"]), (class_in, s["classes"]), (cond_in, s["cond"]), (forward_in, s["forward"]), (cosine_in, s["cosine"]),
        (eigen_x_in, s["eigen_x"]), (eigen_y_in, s["eigen_y"]), (eigen_z_in, s["eigen_z"])])]
    for load in loads:
        load.start()
    barrier = pltpu.get_barrier_semaphore()
    count = greet_halo(barrier) + greet_groups(barrier)
    for load in loads[:3]:
        load.wait()
    fill_field(s["ids"], s["classes"], s["cond"], table_ref, s["field"], s["rows"])
    pl.semaphore_wait(barrier, count)
    copies = halo_copies(s["field"], s["rows"], s["ext"], s["row_ext"], s["halo_send"], s["halo_recv"])
    for copy in copies:
        copy.start()
    for load in loads[3:]:
        load.wait()
    for copy in copies:
        copy.wait()
    heat_part(normals_ref, s["ext"], s["row_ext"], s["forward"], s["s1"], s["root"], s["gain"], s["keep"], s["wa"], s["wb"], s["div"], s["mixed"])
    solve_part(s["s1"], s["forward"], s["cosine"], s["eigen_x"], s["eigen_y"], s["eigen_z"], out_ref, s["r2"], s["s2"], s["r3"], s["s3"],
               s["r4"], s["s4"], s["r5"], s["lines"], s["own_out"], s["peer_out"], s["mixed"],
               s["send_sem"], s["recv_sem"], s["last_send"], s["last_recv"])


def per_device(surface_ids, class_map, conductivity, normals, class_table):
    cosine = cosine_table()
    eigen = eigen_values()
    cosine_pair, forward_pair = jnp.asarray(halves(cosine)), jnp.asarray(halves(cosine.T.copy()))
    eigen_x = jnp.asarray(np.repeat(eigen[:, None], 128, axis=1))
    eigen_y = jnp.asarray(np.repeat(eigen.reshape(16, 16), 16, axis=1))
    eigen_z = jnp.asarray(np.tile(eigen.reshape(16, 16), (1, 16)))
    out = pl.pallas_call(
        whole_kernel,
        out_shape=jax.ShapeDtypeStruct((512, 128), f32),
        in_specs=[pl.BlockSpec(memory_space=pl.ANY)] * 8 + [SM, VM], out_specs=VM,
        scratch_shapes=list(SCRATCH.values()),
        compiler_params=pltpu.CompilerParams(collective_id=0, has_side_effects=True, vmem_limit_bytes=LIMIT),
    )(surface_ids, class_map, conductivity, forward_pair, cosine_pair, eigen_x, eigen_y, eigen_z, class_table, normals)
    return out.reshape(32, 16, 128)


def solution(mesh):
    spec = P("gx", "gy", "gz")
    return jax.shard_map(
        per_device, mesh=mesh, in_specs=(spec, spec, spec, P(), P()), out_specs=spec, check_vma=False
    )
```

```python
import jax
import jax.numpy as jnp
import numpy as np
from jax import lax
from jax.experimental import pallas as pl
from jax.experimental.pallas import tpu as pltpu
from jax.sharding import PartitionSpec as P

N = 256
STEPS = 8
CLASSES = 4
HALO = STEPS + 1
XE = 16 + 2 * HALO
YE = 32
time_step = 0.08
norm_floor = 0.5
f32 = jnp.float32
bf16 = jnp.bfloat16
MESH = pl.DeviceIdType.MESH


def cosine_table():
    wave_number = np.arange(N, dtype=np.float32)[:, None]
    sample = np.arange(N, dtype=np.float32)[None, :]
    factor = np.where(wave_number == 0, np.sqrt(np.float32(1.0 / N)), np.sqrt(np.float32(2.0 / N)))
    angle = np.float32(np.pi) * wave_number * (np.float32(2.0) * sample + np.float32(1.0)) / np.float32(2.0 * N)
    return (factor * np.cos(angle)).astype(np.float32)


def eigen_values():
    wave_number = np.arange(N, dtype=np.float32)
    return (np.float32(2.0) - np.float32(2.0) * np.cos(np.float32(np.pi) * wave_number / np.float32(N))).astype(np.float32)


def halves(table):
    high = table.astype(jnp.bfloat16)
    low = (table - high.astype(np.float32)).astype(jnp.bfloat16)
    return np.stack([high, low])


def split(values):
    high = values.astype(bf16)
    return high, (values - high.astype(f32)).astype(bf16)


def product(left, right):
    dot = lambda a, b: jnp.dot(a, b, preferred_element_type=f32)
    return dot(left[0], right[0]) + (dot(left[1], right[0]) + dot(left[0], right[1]))


def swap8(tile):
    row = lax.broadcasted_iota(jnp.int32, (8, 128), 0)
    group = lax.broadcasted_iota(jnp.int32, (8, 128), 1) // 16
    for bit in (1, 2, 4):
        row_bit = (row // bit) % 2
        group_bit = (group // bit) % 2
        if bit == 4:
            other = pltpu.roll(pltpu.roll(tile, 4, 0), 64, 1)
        else:
            forth = pltpu.roll(pltpu.roll(tile, bit, 0), 128 - 16 * bit, 1)
            back = pltpu.roll(pltpu.roll(tile, 8 - bit, 0), 16 * bit, 1)
            other = jnp.where(row_bit == 1, forth, back)
        tile = jnp.where(row_bit == group_bit, tile, other)
    return tile


BOUNDS = (0, 9, 17, 25, 34)
CHUNKS = ((0, 1), (2,), (3,))


def halo_copies(field, rows, ext, row_ext, send_sem, recv_sem):
    gx, gy, gz = lax.axis_index("gx"), lax.axis_index("gy"), lax.axis_index("gz")
    lanes = pl.ds(pl.multiple_of(gz * 128, 128), 128)
    copies = {}

    def remote(key, src, dst, x, y, core):
        slot = len(copies)
        copies[key] = pltpu.make_async_remote_copy(
            src, dst, send_sem.at[slot], recv_sem.at[slot], device_id=(x, y, core), device_id_type=MESH)

    def face(piece):
        start, size = BOUNDS[piece], BOUNDS[piece + 1] - BOUNDS[piece]
        for dy in (1, -1):
            src_rows, dst_rows = (pl.ds(8, 8), pl.ds(0, 8)) if dy == 1 else (pl.ds(0, 8), pl.ds(24, 8))
            for other in (0, 1):
                core = 1 - gz if other else gz
                if start == 0:
                    first, x = 23 - 16 * core, lax.rem(gx + 1 - core, 8)
                elif start >= 25:
                    first, x = start - 9 - 16 * core, lax.rem(gx - core + 8, 8)
                else:
                    first, x = start - 9 + 16 * core, gx
                remote(("face", piece, dy, other), field.at[:, pl.ds(first, size), src_rows, :],
                       ext.at[:, pl.ds(start, size), dst_rows, lanes], x, lax.rem(gy + dy + 16, 16), core)

    face(0)
    face(1)
    for other in (1, 0):
        core = 1 - gz if other else gz
        remote(("edge", other), field.at[:, pl.ds(23 * (1 - core), 9)], ext.at[:, pl.ds(25 * core, 9), pl.ds(8, 16), lanes],
               lax.rem(gx + 1 - 2 * core + 8, 8), gy, core)
        src, dst = field.at[:, pl.ds(7 * core, 25)], ext.at[:, pl.ds(9 * (1 - core), 25), pl.ds(8, 16), lanes]
        if other:
            remote(("block", 1), src, dst, gx, gy, core)
        else:
            copies["own"] = pltpu.make_async_copy(src, dst, recv_sem.at[len(copies)])
    for side, dy in ((0, 1), (1, -1)):
        for other in (0, 1):
            core = 1 - gz if other else gz
            remote(("row", side, other), rows.at[side, :, pl.ds(pl.multiple_of(16 * core, 16), 16), :],
                   row_ext.at[side, :, :, lanes], gx, lax.rem(gy + dy + 16, 16), core)
    for piece in range(2, len(BOUNDS) - 1):
        face(piece)
    return copies


def greet_halo(barrier):
    gx, gy, gz = lax.axis_index("gx"), lax.axis_index("gy"), lax.axis_index("gz")
    from_x = lax.rem(gx + 2 * gz - 1 + 8, 8)
    count = 0
    for dy in (1, -1, 0):
        y = lax.rem(gy + dy + 16, 16)
        for core in (0, 1):
            pl.semaphore_signal(barrier, inc=1, device_id=(from_x, y, core), device_id_type=MESH)
            count += 1
        pl.semaphore_signal(barrier, inc=1, device_id=(gx, y, 1 - gz), device_id_type=MESH)
        count += 1
        if dy:
            pl.semaphore_signal(barrier, inc=1, device_id=(gx, y, gz), device_id_type=MESH)
            count += 1
    return count


def fill_field(ids_ref, class_ref, cond_ref, table_ref, field, rows):
    def plane(i, _):
        classes = class_ref[i]
        value = jnp.full(classes.shape, table_ref[0], f32)
        for k in range(1, CLASSES):
            value = jnp.where(classes == k, table_ref[k], value)
        field[0, i] = jnp.sqrt(value * cond_ref[i])
        field[1, i] = ids_ref[i].astype(f32)
        return 0
    lax.fori_loop(0, 32, plane, 0)
    for which in range(2):
        rows[0, which] = field[which, :, 7, :]
        rows[1, which] = field[which, :, 8, :]


def lookup(ids_float, tables):
    index = ids_float.astype(jnp.int32) - 1
    low = jnp.bitwise_and(index, 127)
    found = []
    for first, second in tables:
        a = jnp.take_along_axis(first, low, axis=1)
        b = jnp.take_along_axis(second, low, axis=1)
        found.append(jnp.where(index < 0, 0.0, jnp.where(index < 128, a, b)))
    return found


SWAP_UNROLL = 16
UNROLL = 6
UNALIGNED = True
LOOKUP_UNROLL = 4


def z_sum(low, high):
    lane = lax.broadcasted_iota(jnp.int32, low.shape, 1)
    low_up, high_up = pltpu.roll(low, 1, 1), pltpu.roll(high, 1, 1)
    low_down, high_down = pltpu.roll(low, 127, 1), pltpu.roll(high, 127, 1)
    first, last = lane == 0, lane == 127
    return (jnp.where(first, 0.0, low_up) + jnp.where(last, high_down, low_down),
            jnp.where(first, low_up, high_up) + jnp.where(last, 0.0, high_down))


def z_difference(low, high):
    lane = lax.broadcasted_iota(jnp.int32, low.shape, 1)
    low_up, high_up = pltpu.roll(low, 1, 1), pltpu.roll(high, 1, 1)
    low_down, high_down = pltpu.roll(low, 127, 1), pltpu.roll(high, 127, 1)
    first, last = lane == 0, lane == 127
    return (jnp.where(last, high_down, low_down) - jnp.where(first, 0.0, low_up),
            jnp.where(last, 0.0, high_down) - jnp.where(first, low_up, high_up))


BODY = pl.ds(8, YE)


def neighbours(ref, lead, i):
    center = [ref[lead + (h, i, BODY)] for h in range(2)]
    sides = z_sum(*center)
    total = []
    for h in range(2):
        if UNALIGNED:
            y = ref[lead + (h, i, pl.ds(7, YE))] + ref[lead + (h, i, pl.ds(9, YE))]
        else:
            y = pltpu.roll(center[h], 1, 0) + pltpu.roll(center[h], YE - 1, 0)
        x = ref[lead + (h, i - 1, BODY)] + ref[lead + (h, i + 1, BODY)]
        total.append((x + y) + sides[h])
    return center, total


def heat_part(normals_ref, copies, ext, row_ext, forward_ref, out_ref, root, gain, keep, wa, wb, div, mixed):
    gx, gy, gz = lax.axis_index("gx"), lax.axis_index("gy"), lax.axis_index("gz")
    x0 = gx * 32 + gz * 16
    y0 = gy * 16

    def tables(r):
        return [tuple(jnp.broadcast_to(normals_ref[j:j + 1, h * 128:(h + 1) * 128], (r, 128)) for h in range(2)) for j in range(3)]

    def sources(i, parts):
        x = x0 - HALO + i
        x_in = jnp.logical_and(x >= 0, x < N)
        done = []
        for first, count in parts:
            y = lax.broadcasted_iota(jnp.int32, (count, 128), 0) + (y0 - 8 + first)
            inside = jnp.logical_and(jnp.logical_and(y >= 0, y < N), x_in)
            for h in range(2):
                lanes = pl.ds(h * 128, 128)
                value = jnp.where(inside, ext[0, i, pl.ds(first, count), lanes], 0.0)
                found = lookup(ext[1, i, pl.ds(first, count), lanes], tables(count))
                done.append((h, pl.ds(8 + first, count), value, [found[j] * value for j in range(3)]))
        for h, where, value, w in done:
            root[h, i, where] = value
            for j in range(3):
                wa[j, h, i, where] = w[j]

    zero = jnp.zeros((XE, 128), f32)
    for row in (7, 40):
        for h in range(2):
            root[h, :, row, :] = zero
            for j in range(3):
                wa[j, h, :, row, :] = zero
                wb[j, h, :, row, :] = zero

    for key in (("block", 1), ("edge", 1), ("edge", 0), "own"):
        copies[key].wait()

    def middle(i, _):
        sources(i, [(8, 16)])
        return 0
    lax.fori_loop(0, XE, middle, 0, unroll=LOOKUP_UNROLL)

    for side, dy in ((0, 1), (1, -1)):
        for other in (0, 1):
            copies[("row", side, other)].wait()
    for side in range(2):
        y = y0 - 9 if side == 0 else y0 + 24
        y_in = jnp.logical_and(y >= 0, y < N)
        row = 7 if side == 0 else 40
        for h in range(2):
            lanes = pl.ds(h * 128, 128)
            value = jnp.where(y_in, row_ext[side, 0, :, lanes], 0.0)
            found = lookup(row_ext[side, 1, :, lanes], tables(16))
            root[h, pl.ds(9, 16), row, :] = value
            for j in range(3):
                wa[j, h, pl.ds(9, 16), row, :] = found[j] * value

    def sides(i, _):
        sources(i, [(0, 8), (24, 8)])
        return 0

    def coefficients(i, _):
        center, total = neighbours(root, (), i)
        for h in range(2):
            keep[h, i] = 1.0 - time_step * center[h] * total[h]
            gain[h, i] = time_step * center[h] * center[h]
        return 0

    def plane(src, dst):
        def body(i, _):
            done = []
            for j in range(3):
                center, total = neighbours(src, (j,), i)
                for h in range(2):
                    done.append((j, h, keep[h, i] * center[h] + gain[h, i] * total[h]))
            for j, h, value in done:
                dst[j, h, i, BODY] = value
            return 0
        return body

    def unit(i, _):
        for h in range(2):
            w = [wa[j, h, i, BODY] for j in range(3)]
            size = jnp.sqrt(w[0] * w[0] + w[1] * w[1] + w[2] * w[2])
            floor = jnp.maximum(jnp.maximum(size, norm_floor * root[h, i, BODY]), 1e-30)
            scale = 0.5 / floor
            for j in range(3):
                wb[j, h, i, BODY] = w[j] * scale
        return 0

    before = 0
    for pieces in CHUNKS:
        reach = BOUNDS[pieces[-1] + 1]
        for piece in pieces:
            for dy in (1, -1):
                for other in (0, 1):
                    copies[("face", piece, dy, other)].wait()
        lax.fori_loop(before, reach, sides, 0, unroll=LOOKUP_UNROLL)
        lax.fori_loop(max(1, before - 1), reach - 1, coefficients, 0, unroll=UNROLL)
        if before < 2 * STEPS + 1:
            for step in range(1, STEPS + 1):
                first, end = max(step, before - step), reach - step
                src, dst = (wa, wb) if step % 2 else (wb, wa)
                if first < end:
                    lax.fori_loop(first, end, plane(src, dst), 0, unroll=min(UNROLL, end - first))
        else:
            def pair(p, _, before=before, reach=reach):
                for odd, src, dst in ((1, wa, wb), (2, wb, wa)):
                    first = before - odd - 2 * p
                    body = plane(src, dst)
                    for k in range(reach - before):
                        body(first + k, 0)
                return 0
            lax.fori_loop(0, STEPS // 2, pair, 0)
        first = max(STEPS, before - STEPS - 1)
        end = XE - STEPS if reach == XE else reach - STEPS - 1
        if first < end:
            lax.fori_loop(first, end, unit, 0, unroll=min(UNROLL, end - first))
        before = reach

    def divergence(k, _):
        i = k + HALO
        part_z = z_difference(*[wb[2, h, i, pl.ds(16, 16)] for h in range(2)])
        for h in range(2):
            part_x = wb[0, h, i + 1, pl.ds(16, 16)] - wb[0, h, i - 1, pl.ds(16, 16)]
            part_y = wb[1, h, i, pl.ds(17, 16)] - wb[1, h, i, pl.ds(15, 16)]
            div[h, pl.ds(pl.multiple_of(k * 16, 16), 16), :] = part_x + part_y + part_z[h]
        return 0
    lax.fori_loop(0, 16, divergence, 0, unroll=4)

    lines = jnp.concatenate(
        [jnp.concatenate([div[h, pl.ds(y, 16, stride=16), :] for y in range(16)], axis=0) for h in range(2)], axis=1)
    mixed[...] = product(split(lines), (forward_ref[0], forward_ref[1]))

    def spread(y, _):
        for xh in range(2):
            for ah in range(2):
                tile = mixed[pl.ds(pl.multiple_of(y * 16 + xh * 8, 8), 8), pl.ds(ah * 128, 128)]
                out_ref[xh, pl.ds(ah * 128 + y, 8, stride=16), :] = swap8(tile)
        return 0
    lax.fori_loop(0, 16, spread, 0, unroll=SWAP_UNROLL)


def y_group(index):
    return (lax.axis_index("gx"), index, lax.axis_index("gz"))


def x_group(index):
    return (index // 2, lax.axis_index("gy"), index % 2)


def exchange(src, dst, me, where, send_sem, recv_sem):
    def copy(d):
        to = lax.rem(me + d, 16)
        return pltpu.make_async_remote_copy(
            src.at[:, pl.ds(pl.multiple_of(to * 16, 16), 16), :],
            dst.at[:, pl.ds(pl.multiple_of(me * 16, 16), 16), :],
            send_sem.at[d], recv_sem.at[d], device_id=where(to), device_id_type=MESH)

    def start(d, _):
        copy(d).start()
        return 0
    lax.fori_loop(1, 16, start, 0)
    own = pl.ds(pl.multiple_of(me * 16, 16), 16)
    dst[:, own, :] = src[:, own, :]

    def wait(d, _):
        copy(d).wait()
        return 0
    lax.fori_loop(1, 16, wait, 0)


def whole(ref):
    return jnp.concatenate([ref[0], ref[1]], axis=1)


def turn(values, mixed, dst):
    mixed[...] = values

    def block(b, _):
        for rh in range(2):
            for gh in range(2):
                tile = mixed[pl.ds(pl.multiple_of(b * 16 + rh * 8, 8), 8), pl.ds(gh * 128, 128)]
                dst[rh, pl.ds(pl.multiple_of(b * 16 + gh * 8, 8), 8), :] = swap8(tile)
        return 0
    lax.fori_loop(0, 16, block, 0, unroll=SWAP_UNROLL)


def greet_groups(barrier):
    gx, gy, gz = lax.axis_index("gx"), lax.axis_index("gy"), lax.axis_index("gz")
    group = gx * 2 + gz

    def greet(d, _):
        pl.semaphore_signal(barrier, inc=1, device_id=y_group(lax.rem(gy + d, 16)), device_id_type=MESH)
        pl.semaphore_signal(barrier, inc=1, device_id=x_group(lax.rem(group + d, 16)), device_id_type=MESH)
        return 0
    lax.fori_loop(1, 16, greet, 0)
    return 30


def solve_part(s1, forward_ref, cosine_ref, eigen_x, eigen_y, eigen_z, out_ref, r2, s2, r3, s3, r4, s4, r5, lines, own_out, peer_out, mixed,
               send_sem, recv_sem, last_send, last_recv):
    gx, gy, gz = lax.axis_index("gx"), lax.axis_index("gy"), lax.axis_index("gz")
    group = gx * 2 + gz
    cosine = (cosine_ref[0], cosine_ref[1])
    forward = (forward_ref[0], forward_ref[1])
    exchange(s1, r2, gy, y_group, send_sem.at[0], recv_sem.at[0])
    turn(product(cosine, split(whole(r2))), mixed, s2)
    exchange(s2, r3, group, x_group, send_sem.at[1], recv_sem.at[1])
    spectrum = product(cosine, split(whole(r3)))
    rest = eigen_y[pl.ds(group, 1), :] + eigen_z[pl.ds(gy, 1), :]
    eigen = jnp.concatenate([eigen_x[...], eigen_x[...]], axis=1)
    solved = -spectrum / (eigen + rest + 4.0 / (N * N))
    turn(product(forward, split(solved)), mixed, s3)
    exchange(s3, r4, group, x_group, send_sem.at[2], recv_sem.at[2])
    values = product(forward, split(whole(r4)))
    for h in range(2):
        s4[h] = values[:, h * 128:(h + 1) * 128]
    exchange(s4, r5, gy, y_group, send_sem.at[3], recv_sem.at[3])

    def gather(y, _):
        for xh in range(2):
            for ah in range(2):
                tile = r5[xh, pl.ds(ah * 128 + y, 8, stride=16), :]
                lines[pl.ds(pl.multiple_of(y * 16 + xh * 8, 8), 8), pl.ds(ah * 128, 128)] = swap8(tile)
        return 0
    lax.fori_loop(0, 16, gather, 0, unroll=SWAP_UNROLL)
    values = product(split(lines[...]), cosine)
    first = gz == 0
    mine = jnp.where(first, values[:, :128], values[:, 128:])
    theirs = jnp.where(first, values[:, 128:], values[:, :128])
    for y in range(16):
        peer_out[pl.ds(y, 16, stride=16), :] = theirs[y * 16:(y + 1) * 16]
    rows = pl.ds(pl.multiple_of(gz * 256, 256), 256)
    copy = pltpu.make_async_remote_copy(
        peer_out, out_ref.at[rows, :], last_send, last_recv, device_id=(gx, gy, 1 - gz), device_id_type=MESH)
    copy.start()
    for y in range(16):
        own_out[pl.ds(y, 16, stride=16), :] = mine[y * 16:(y + 1) * 16]
    out_ref[rows, :] = own_out[...]
    copy.wait()


VM = pl.BlockSpec(memory_space=pltpu.VMEM)
SM = pl.BlockSpec(memory_space=pltpu.SMEM)
DMA = pltpu.SemaphoreType.DMA
LIMIT = 62 * 1024 * 1024


def vmem(*shape):
    return pltpu.VMEM(shape, f32)


SCRATCH = dict(
    ids=pltpu.VMEM((32, 16, 128), jnp.int32), classes=pltpu.VMEM((32, 16, 128), jnp.int32), cond=vmem(32, 16, 128),
    forward=pltpu.VMEM((2, 256, 256), bf16), cosine=pltpu.VMEM((2, 256, 256), bf16),
    eigen_x=vmem(256, 128), eigen_y=vmem(16, 256), eigen_z=vmem(16, 256), in_sem=DMA((8,)),
    field=vmem(2, 32, 16, 128), rows=vmem(2, 2, 32, 128), ext=vmem(2, XE, YE, 256), row_ext=vmem(2, 2, 16, 256),
    halo_send=DMA((40,)), halo_recv=DMA((40,)),
    root=vmem(2, XE, 48, 128), gain=vmem(2, XE, YE, 128), keep=vmem(2, XE, YE, 128),
    wa=vmem(3, 2, XE, 48, 128), wb=vmem(3, 2, XE, 48, 128), div=vmem(2, 256, 128), mixed=vmem(256, 256),
    s1=vmem(2, 256, 128), r2=vmem(2, 256, 128), s2=vmem(2, 256, 128), r3=vmem(2, 256, 128), s3=vmem(2, 256, 128),
    r4=vmem(2, 256, 128), s4=vmem(2, 256, 128), r5=vmem(2, 256, 128), lines=vmem(256, 256),
    own_out=vmem(256, 128), peer_out=vmem(256, 128),
    send_sem=DMA((4, 16)), recv_sem=DMA((4, 16)), last_send=DMA(()), last_recv=DMA(()),
)


def whole_kernel(ids_in, class_in, cond_in, forward_in, cosine_in, eigen_x_in, eigen_y_in, eigen_z_in, table_ref, normals_ref, out_ref, *scratch):
    s = dict(zip(SCRATCH, scratch))
    loads = [pltpu.make_async_copy(src, dst, s["in_sem"].at[k]) for k, (src, dst) in enumerate([
        (ids_in, s["ids"]), (class_in, s["classes"]), (cond_in, s["cond"]), (forward_in, s["forward"]), (cosine_in, s["cosine"]),
        (eigen_x_in, s["eigen_x"]), (eigen_y_in, s["eigen_y"]), (eigen_z_in, s["eigen_z"])])]
    for load in loads:
        load.start()
    barrier = pltpu.get_barrier_semaphore()
    count = greet_halo(barrier) + greet_groups(barrier)
    for load in loads[:3]:
        load.wait()
    fill_field(s["ids"], s["classes"], s["cond"], table_ref, s["field"], s["rows"])
    pl.semaphore_wait(barrier, count)
    copies = halo_copies(s["field"], s["rows"], s["ext"], s["row_ext"], s["halo_send"], s["halo_recv"])
    for copy in copies.values():
        copy.start()
    for load in loads[3:]:
        load.wait()
    heat_part(normals_ref, copies, s["ext"], s["row_ext"], s["forward"], s["s1"], s["root"], s["gain"], s["keep"], s["wa"], s["wb"], s["div"], s["mixed"])
    solve_part(s["s1"], s["forward"], s["cosine"], s["eigen_x"], s["eigen_y"], s["eigen_z"], out_ref, s["r2"], s["s2"], s["r3"], s["s3"],
               s["r4"], s["s4"], s["r5"], s["lines"], s["own_out"], s["peer_out"], s["mixed"],
               s["send_sem"], s["recv_sem"], s["last_send"], s["last_recv"])


def per_device(surface_ids, class_map, conductivity, normals, class_table):
    cosine = cosine_table()
    eigen = eigen_values()
    cosine_pair, forward_pair = jnp.asarray(halves(cosine)), jnp.asarray(halves(cosine.T.copy()))
    eigen_x = jnp.asarray(np.repeat(eigen[:, None], 128, axis=1))
    eigen_y = jnp.asarray(np.repeat(eigen.reshape(16, 16), 16, axis=1))
    eigen_z = jnp.asarray(np.tile(eigen.reshape(16, 16), (1, 16)))
    out = pl.pallas_call(
        whole_kernel,
        out_shape=jax.ShapeDtypeStruct((512, 128), f32),
        in_specs=[pl.BlockSpec(memory_space=pltpu.HBM)] * 8 + [SM, VM], out_specs=VM,
        scratch_shapes=list(SCRATCH.values()),
        compiler_params=pltpu.CompilerParams(collective_id=0, has_side_effects=True, vmem_limit_bytes=LIMIT),
    )(surface_ids, class_map, conductivity, forward_pair, cosine_pair, eigen_x, eigen_y, eigen_z, class_table, normals)
    return out.reshape(32, 16, 128)


def solution(mesh):
    spec = P("gx", "gy", "gz")
    return jax.shard_map(
        per_device, mesh=mesh, in_specs=(spec, spec, spec, P(), P()), out_specs=spec, check_vma=False
    )
```

```python
import jax
import jax.numpy as jnp
import numpy as np
from jax import lax
from jax.experimental import pallas as pl
from jax.experimental.pallas import tpu as pltpu
from jax.sharding import PartitionSpec as P

N = 256
STEPS = 8
CLASSES = 4
HALO = STEPS + 1
XE = 16 + 2 * HALO
YE = 32
time_step = 0.08
norm_floor = 0.5
f32 = jnp.float32
bf16 = jnp.bfloat16
MESH = pl.DeviceIdType.MESH


def cosine_table():
    wave_number = np.arange(N, dtype=np.float32)[:, None]
    sample = np.arange(N, dtype=np.float32)[None, :]
    factor = np.where(wave_number == 0, np.sqrt(np.float32(1.0 / N)), np.sqrt(np.float32(2.0 / N)))
    angle = np.float32(np.pi) * wave_number * (np.float32(2.0) * sample + np.float32(1.0)) / np.float32(2.0 * N)
    return (factor * np.cos(angle)).astype(np.float32)


def eigen_values():
    wave_number = np.arange(N, dtype=np.float32)
    return (np.float32(2.0) - np.float32(2.0) * np.cos(np.float32(np.pi) * wave_number / np.float32(N))).astype(np.float32)


def halves(table):
    high = table.astype(jnp.bfloat16)
    low = (table - high.astype(np.float32)).astype(jnp.bfloat16)
    return np.stack([high, low])


def split(values):
    high = values.astype(bf16)
    return high, (values - high.astype(f32)).astype(bf16)


def product(left, right):
    dot = lambda a, b: jnp.dot(a, b, preferred_element_type=f32)
    return dot(left[0], right[0]) + (dot(left[1], right[0]) + dot(left[0], right[1]))


def swap8(tile):
    row = lax.broadcasted_iota(jnp.int32, (8, 128), 0)
    group = lax.broadcasted_iota(jnp.int32, (8, 128), 1) // 16
    for bit in (1, 2, 4):
        row_bit = (row // bit) % 2
        group_bit = (group // bit) % 2
        if bit == 4:
            other = pltpu.roll(pltpu.roll(tile, 4, 0), 64, 1)
        else:
            forth = pltpu.roll(pltpu.roll(tile, bit, 0), 128 - 16 * bit, 1)
            back = pltpu.roll(pltpu.roll(tile, 8 - bit, 0), 16 * bit, 1)
            other = jnp.where(row_bit == 1, forth, back)
        tile = jnp.where(row_bit == group_bit, tile, other)
    return tile


INNER = ((7, 9), (16, 9))
OUTER = ((0, 7), (25, 7))
MARCH = True


def halo_copies(field, rows, ext, row_ext, send_sem, recv_sem):
    gx, gy, gz = lax.axis_index("gx"), lax.axis_index("gy"), lax.axis_index("gz")
    lanes = pl.ds(pl.multiple_of(gz * 128, 128), 128)
    copies = {}

    def remote(key, src, dst, x, y, core):
        slot = len(copies)
        copies[key] = pltpu.make_async_remote_copy(
            src, dst, send_sem.at[slot], recv_sem.at[slot], device_id=(x, y, core), device_id_type=MESH)

    def next_y(dy):
        return lax.rem(gy + dy + 16, 16)

    def next_x(core):
        return lax.rem(gx + 1 - 2 * core + 8, 8)

    for first, size in INNER + OUTER:
        for dy in (1, -1):
            src_rows, dst_rows = (pl.ds(8, 8), pl.ds(0, 8)) if dy == 1 else (pl.ds(0, 8), pl.ds(24, 8))
            place = ext.at[:, pl.ds(9 + first, size), dst_rows, lanes]
            remote(("face", first, dy), field.at[:, pl.ds(first, size), src_rows, :], place, gx, next_y(dy), gz)
            if (first, size) in INNER:
                remote(("pass", first, dy), place, place, gx, gy, 1 - gz)
    for dy in (1, -1):
        dst_rows = pl.ds(0, 8) if dy == 1 else pl.ds(24, 8)
        place = ext.at[:, pl.ds(9 + 25 * (1 - gz), 7), dst_rows, lanes]
        remote(("pass", "outer", dy), place, place, gx, gy, 1 - gz)
        for other in (0, 1):
            core = 1 - gz if other else gz
            remote(("corner", other, dy), ext.at[:, pl.ds(9 + 23 * (1 - core), 9), dst_rows, lanes],
                   ext.at[:, pl.ds(41 * core, 9), dst_rows, lanes], next_x(core), gy, core)
    middle_rows = pl.ds(8, 16)
    for other in (1, 0):
        core = 1 - gz if other else gz
        remote(("edge", other), field.at[:, pl.ds(23 * (1 - core), 9)], ext.at[:, pl.ds(41 * core, 9), middle_rows, lanes],
               next_x(core), gy, core)
        src, dst = field.at[:, pl.ds(7 * core, 25)], ext.at[:, pl.ds(9 + 7 * core, 25), middle_rows, lanes]
        if other:
            remote(("block", 1), src, dst, gx, gy, core)
        else:
            copies["own"] = pltpu.make_async_copy(src, dst, recv_sem.at[len(copies)])
    for side, dy in ((0, 1), (1, -1)):
        for other in (0, 1):
            core = 1 - gz if other else gz
            remote(("row", side, other), rows.at[side, :, pl.ds(pl.multiple_of(16 * core, 16), 16), :],
                   row_ext.at[side, :, :, lanes], gx, next_y(dy), core)
    return copies


def start_all(copies, *kinds):
    for kind in kinds:
        for key, copy in copies.items():
            if key == kind or key[:len(kind)] == kind:
                copy.start()


def wait_all(copies, *kinds):
    for kind in kinds:
        for key, copy in copies.items():
            if key == kind or key[:len(kind)] == kind:
                copy.wait()


def greet_halo(barrier):
    gx, gy, gz = lax.axis_index("gx"), lax.axis_index("gy"), lax.axis_index("gz")
    from_x = lax.rem(gx + 2 * gz - 1 + 8, 8)
    others = [(gx, lax.rem(gy + dy + 16, 16), core) for dy in (1, -1) for core in (0, 1)]
    others += [(gx, gy, 1 - gz), (from_x, gy, 0), (from_x, gy, 1)]
    for other in others:
        pl.semaphore_signal(barrier, inc=1, device_id=other, device_id_type=MESH)
    return len(others)


def fill_field(ids_ref, class_ref, cond_ref, table_ref, field, rows):
    lane = lax.broadcasted_iota(jnp.int32, (16, 128), 1)
    odd_first = lax.axis_index("gz")
    order = 2 * (lane % 64) + jnp.where(lane < 64, odd_first, 1 - odd_first)

    def plane(i, _):
        classes = class_ref[i]
        value = jnp.full(classes.shape, table_ref[0], f32)
        for k in range(1, CLASSES):
            value = jnp.where(classes == k, table_ref[k], value)
        root = jnp.sqrt(value * cond_ref[i])
        field[0, i] = jnp.take_along_axis(root, order, axis=1)
        field[1, i] = jnp.take_along_axis(ids_ref[i].astype(f32), order, axis=1)
        return 0
    lax.fori_loop(0, 32, plane, 0, unroll=4)
    for which in range(2):
        rows[0, which] = field[which, :, 7, :]
        rows[1, which] = field[which, :, 8, :]


def even_odd(first, second):
    low = lax.broadcasted_iota(jnp.int32, first.shape, 1) < 64
    return jnp.where(low, first, second), pltpu.roll(jnp.where(low, second, first), 64, 1)


def lookup(ids_float, tables):
    index = ids_float.astype(jnp.int32) - 1
    low = jnp.bitwise_and(index, 127)
    found = []
    for first, second in tables:
        a = jnp.take_along_axis(first, low, axis=1)
        b = jnp.take_along_axis(second, low, axis=1)
        found.append(jnp.where(index < 0, 0.0, jnp.where(index < 128, a, b)))
    return found


SWAP_UNROLL = 16
UNROLL = 6
UNALIGNED = True
LOOKUP_UNROLL = 4


def z_sides(even, odd):
    lane = lax.broadcasted_iota(jnp.int32, even.shape, 1)
    return jnp.where(lane == 0, 0.0, pltpu.roll(odd, 1, 1)), jnp.where(lane == 127, 0.0, pltpu.roll(even, 127, 1))


def z_sum(even, odd):
    before, after = z_sides(even, odd)
    return before + odd, even + after


def z_difference(even, odd):
    before, after = z_sides(even, odd)
    return odd - before, after - even


BODY = pl.ds(8, YE)


def neighbours(ref, lead, i):
    center = [ref[lead + (h, i, BODY)] for h in range(2)]
    sides = z_sum(*center)
    total = []
    for h in range(2):
        if UNALIGNED:
            y = ref[lead + (h, i, pl.ds(7, YE))] + ref[lead + (h, i, pl.ds(9, YE))]
        else:
            y = pltpu.roll(center[h], 1, 0) + pltpu.roll(center[h], YE - 1, 0)
        x = ref[lead + (h, i - 1, BODY)] + ref[lead + (h, i + 1, BODY)]
        total.append((x + y) + sides[h])
    return center, total


def heat_part(normals_ref, copies, ext, row_ext, forward_ref, out_ref, root, gain, keep, wa, wb, row_w, div, mixed):
    gx, gy, gz = lax.axis_index("gx"), lax.axis_index("gy"), lax.axis_index("gz")
    y0 = gy * 16

    def tables(r):
        return [tuple(jnp.broadcast_to(normals_ref[j:j + 1, h * 128:(h + 1) * 128], (r, 128)) for h in range(2)) for j in range(3)]

    def sources(m, parts):
        p = 33 - m + gz * (2 * m - 17)
        x = gx * 32 - HALO + p
        x_in = jnp.logical_and(x >= 0, x < N)
        done = []
        for first, count in parts:
            y = lax.broadcasted_iota(jnp.int32, (count, 128), 0) + (y0 - 8 + first)
            inside = jnp.logical_and(jnp.logical_and(y >= 0, y < N), x_in)
            both = [even_odd(*[ext[a, p, pl.ds(first, count), pl.ds(c * 128, 128)] for c in range(2)]) for a in range(2)]
            for h in range(2):
                value = jnp.where(inside, both[0][h], 0.0)
                found = lookup(both[1][h], tables(count))
                done.append((h, pl.ds(8 + first, count), value, [found[j] * value for j in range(3)]))
        for h, where, value, w in done:
            root[h, m, where] = value
            for j in range(3):
                wa[j, h, m, where] = w[j]

    def middle(m, _):
        sources(m, [(8, 16)])
        return 0

    def sides(m, _):
        sources(m, [(0, 8), (24, 8)])
        return 0

    def coefficients(m, _):
        center, total = neighbours(root, (), m)
        for h in range(2):
            keep[h, m] = 1.0 - time_step * center[h] * total[h]
            gain[h, m] = time_step * center[h] * center[h]
        return 0

    def march(src, dst, first, count):
        if not MARCH:
            for k in range(count):
                m = first + k
                done = []
                for j in range(3):
                    center, total = neighbours(src, (j,), m)
                    for h in range(2):
                        done.append((j, h, keep[h, m] * center[h] + gain[h, m] * total[h]))
                for j, h, value in done:
                    dst[j, h, m, BODY] = value
            return
        pairs = [(j, h) for j in range(3) for h in range(2)]
        for r in range(YE // 8):
            here, above, below = pl.ds(8 + 8 * r, 8), pl.ds(7 + 8 * r, 8), pl.ds(9 + 8 * r, 8)
            last = {q: src[q + (first - 1, here)] for q in pairs}
            now = {q: src[q + (first, here)] for q in pairs}
            for k in range(count):
                m = first + k
                coming = {q: src[q + (m + 1, here)] for q in pairs}
                scale = [(keep[h, m, pl.ds(8 * r, 8)], gain[h, m, pl.ds(8 * r, 8)]) for h in range(2)]
                done = {}
                for j in range(3):
                    z = z_sum(now[j, 0], now[j, 1])
                    for h in range(2):
                        q = (j, h)
                        y = src[q + (m, above)] + src[q + (m, below)]
                        done[q] = scale[h][0] * now[q] + scale[h][1] * ((last[q] + coming[q]) + (y + z[h]))
                for q in pairs:
                    dst[q + (m, here)] = done[q]
                last, now = now, coming

    def unit(m, _):
        for h in range(2):
            w = [wa[j, h, m, BODY] for j in range(3)]
            size = jnp.sqrt(w[0] * w[0] + w[1] * w[1] + w[2] * w[2])
            floor = jnp.maximum(jnp.maximum(size, norm_floor * root[h, m, BODY]), 1e-30)
            scale = 0.5 / floor
            for j in range(3):
                wb[j, h, m, BODY] = w[j] * scale
        return 0

    def looked_up(body, first, end):
        lax.fori_loop(first, end, body, 0, unroll=LOOKUP_UNROLL)

    zero = jnp.zeros((XE, 128), f32)
    for row in (7, 40):
        for h in range(2):
            root[h, :, row, :] = zero
            for j in range(3):
                wa[j, h, :, row, :] = zero
                wb[j, h, :, row, :] = zero

    wait_all(copies, "own", ("block",))
    looked_up(middle, 0, 12)
    for first, _ in INNER:
        for dy in (1, -1):
            copies["face", first, dy].wait()
            copies["pass", first, dy].start()
    looked_up(middle, 12, 25)
    wait_all(copies, ("row",))
    for side in range(2):
        y = y0 - 9 if side == 0 else y0 + 24
        y_in = jnp.logical_and(y >= 0, y < N)
        both = [even_odd(*[row_ext[side, a, :, pl.ds(c * 128, 128)] for c in range(2)]) for a in range(2)]
        for h in range(2):
            value = jnp.where(y_in, both[0][h], 0.0)
            found = lookup(both[1][h], tables(16))
            row_w[side, h, 3] = value
            for j in range(3):
                row_w[side, h, j] = found[j] * value

    def outer_row(m, _):
        k = 24 - m + gz * (2 * m - 33)
        for side, row in ((0, 7), (1, 40)):
            for h in range(2):
                root[h, m, pl.ds(row, 1)] = row_w[side, h, 3, pl.ds(k, 1)]
                for j in range(3):
                    wa[j, h, m, pl.ds(row, 1)] = row_w[side, h, j, pl.ds(k, 1)]
        return 0
    lax.fori_loop(9, 25, outer_row, 0, unroll=4)

    for before, reach in ((0, 18), (18, 25), (25, XE)):
        if before == 0:
            wait_all(copies, ("pass", INNER[0][0]), ("pass", INNER[1][0]))
        elif before == 18:
            wait_all(copies, ("pass", "outer"))
        else:
            wait_all(copies, ("edge",), ("corner",))
            looked_up(middle, before, reach)
        looked_up(sides, before, reach)
        lax.fori_loop(max(1, before - 1), reach - 1, coefficients, 0, unroll=UNROLL)
        if before == 0:
            for first, _ in OUTER:
                for dy in (1, -1):
                    copies["face", first, dy].wait()
            start_all(copies, ("pass", "outer"), ("corner",))
            for step in range(1, STEPS + 1):
                src, dst = (wa, wb) if step % 2 else (wb, wa)
                march(src, dst, step, reach - 2 * step)
        else:
            def pair(p, _, before=before, reach=reach):
                for odd, src, dst in ((1, wa, wb), (2, wb, wa)):
                    march(src, dst, before - odd - 2 * p, reach - before)
                return 0
            lax.fori_loop(0, STEPS // 2, pair, 0)
        first = max(STEPS, before - STEPS - 1)
        end = XE - STEPS if reach == XE else reach - STEPS - 1
        lax.fori_loop(first, end, unit, 0, unroll=min(UNROLL, end - first))

    sign = (2 * gz - 1).astype(f32)

    def divergence(k, _):
        m = 24 - k + gz * (2 * k - 15)
        part_z = z_difference(*[wb[2, h, m, pl.ds(16, 16)] for h in range(2)])
        for h in range(2):
            part_x = sign * (wb[0, h, m + 1, pl.ds(16, 16)] - wb[0, h, m - 1, pl.ds(16, 16)])
            part_y = wb[1, h, m, pl.ds(17, 16)] - wb[1, h, m, pl.ds(15, 16)]
            div[h, pl.ds(pl.multiple_of(k * 16, 16), 16), :] = part_x + part_y + part_z[h]
        return 0
    lax.fori_loop(0, 16, divergence, 0, unroll=4)

    lines = jnp.concatenate(
        [jnp.concatenate([div[h, pl.ds(y, 16, stride=16), :] for y in range(16)], axis=0) for h in range(2)], axis=1)
    mixed[...] = product(split(lines), (forward_ref[0], forward_ref[1]))

    def spread(y, _):
        for xh in range(2):
            for ah in range(2):
                tile = mixed[pl.ds(pl.multiple_of(y * 16 + xh * 8, 8), 8), pl.ds(ah * 128, 128)]
                out_ref[xh, pl.ds(ah * 128 + y, 8, stride=16), :] = swap8(tile)
        return 0
    lax.fori_loop(0, 16, spread, 0, unroll=SWAP_UNROLL)


def y_group(index):
    return (lax.axis_index("gx"), index, lax.axis_index("gz"))


def x_group(index):
    return (index // 2, lax.axis_index("gy"), index % 2)


def exchange(src, dst, me, where, send_sem, recv_sem):
    def copy(d):
        to = lax.rem(me + d, 16)
        return pltpu.make_async_remote_copy(
            src.at[:, pl.ds(pl.multiple_of(to * 16, 16), 16), :],
            dst.at[:, pl.ds(pl.multiple_of(me * 16, 16), 16), :],
            send_sem.at[d], recv_sem.at[d], device_id=where(to), device_id_type=MESH)

    for d in (8, 7, 9, 6, 10, 5, 11, 4, 12, 3, 13, 2, 14, 1, 15):
        copy(d).start()
    own = pl.ds(pl.multiple_of(me * 16, 16), 16)
    dst[:, own, :] = src[:, own, :]

    for d in range(1, 16):
        copy(d).wait()


def whole(ref):
    return jnp.concatenate([ref[0], ref[1]], axis=1)


def turn(values, mixed, dst):
    mixed[...] = values

    def block(b, _):
        for rh in range(2):
            for gh in range(2):
                tile = mixed[pl.ds(pl.multiple_of(b * 16 + rh * 8, 8), 8), pl.ds(gh * 128, 128)]
                dst[rh, pl.ds(pl.multiple_of(b * 16 + gh * 8, 8), 8), :] = swap8(tile)
        return 0
    lax.fori_loop(0, 16, block, 0, unroll=SWAP_UNROLL)


def greet_groups(barrier):
    gx, gy, gz = lax.axis_index("gx"), lax.axis_index("gy"), lax.axis_index("gz")
    group = gx * 2 + gz

    def greet(d, _):
        pl.semaphore_signal(barrier, inc=1, device_id=y_group(lax.rem(gy + d, 16)), device_id_type=MESH)
        pl.semaphore_signal(barrier, inc=1, device_id=x_group(lax.rem(group + d, 16)), device_id_type=MESH)
        return 0
    lax.fori_loop(1, 16, greet, 0)
    return 30


def solve_part(s1, forward_ref, cosine_ref, eigen_x, eigen_y, eigen_z, out_ref, r2, s2, r3, s3, r4, s4, r5, lines, own_out, peer_out, mixed,
               send_sem, recv_sem, last_send, last_recv):
    gx, gy, gz = lax.axis_index("gx"), lax.axis_index("gy"), lax.axis_index("gz")
    group = gx * 2 + gz
    cosine = (cosine_ref[0], cosine_ref[1])
    forward = (forward_ref[0], forward_ref[1])
    exchange(s1, r2, gy, y_group, send_sem.at[0], recv_sem.at[0])
    turn(product(cosine, split(whole(r2))), mixed, s2)
    exchange(s2, r3, group, x_group, send_sem.at[1], recv_sem.at[1])
    spectrum = product(cosine, split(whole(r3)))
    rest = eigen_y[pl.ds(group, 1), :] + eigen_z[pl.ds(gy, 1), :]
    eigen = jnp.concatenate([eigen_x[...], eigen_x[...]], axis=1)
    solved = -spectrum / (eigen + rest + 4.0 / (N * N))
    turn(product(forward, split(solved)), mixed, s3)
    exchange(s3, r4, group, x_group, send_sem.at[2], recv_sem.at[2])
    values = product(forward, split(whole(r4)))
    for h in range(2):
        s4[h] = values[:, h * 128:(h + 1) * 128]
    exchange(s4, r5, gy, y_group, send_sem.at[3], recv_sem.at[3])

    def gather(y, _):
        for xh in range(2):
            for ah in range(2):
                tile = r5[xh, pl.ds(ah * 128 + y, 8, stride=16), :]
                lines[pl.ds(pl.multiple_of(y * 16 + xh * 8, 8), 8), pl.ds(ah * 128, 128)] = swap8(tile)
        return 0
    lax.fori_loop(0, 16, gather, 0, unroll=SWAP_UNROLL)
    values = product(split(lines[...]), cosine)
    first = gz == 0
    mine = jnp.where(first, values[:, :128], values[:, 128:])
    theirs = jnp.where(first, values[:, 128:], values[:, :128])
    for y in range(16):
        peer_out[pl.ds(y, 16, stride=16), :] = theirs[y * 16:(y + 1) * 16]
    rows = pl.ds(pl.multiple_of(gz * 256, 256), 256)
    copy = pltpu.make_async_remote_copy(
        peer_out, out_ref.at[rows, :], last_send, last_recv, device_id=(gx, gy, 1 - gz), device_id_type=MESH)
    copy.start()
    for y in range(16):
        own_out[pl.ds(y, 16, stride=16), :] = mine[y * 16:(y + 1) * 16]
    out_ref[rows, :] = own_out[...]
    copy.wait()


VM = pl.BlockSpec(memory_space=pltpu.VMEM)
SM = pl.BlockSpec(memory_space=pltpu.SMEM)
DMA = pltpu.SemaphoreType.DMA
LIMIT = 62 * 1024 * 1024


def vmem(*shape):
    return pltpu.VMEM(shape, f32)


SCRATCH = dict(
    ids=pltpu.VMEM((32, 16, 128), jnp.int32), classes=pltpu.VMEM((32, 16, 128), jnp.int32), cond=vmem(32, 16, 128),
    first=pltpu.VMEM((2, 256, 256), bf16), forward=pltpu.VMEM((2, 256, 256), bf16), cosine=pltpu.VMEM((2, 256, 256), bf16),
    eigen_x=vmem(256, 128), eigen_y=vmem(16, 256), eigen_z=vmem(16, 256), in_sem=DMA((9,)),
    field=vmem(2, 32, 16, 128), rows=vmem(2, 2, 32, 128), ext=vmem(2, 50, YE, 256), row_ext=vmem(2, 2, 16, 256),
    halo_send=DMA((40,)), halo_recv=DMA((40,)),
    root=vmem(2, XE, 48, 128), gain=vmem(2, XE, YE, 128), keep=vmem(2, XE, YE, 128),
    wa=vmem(3, 2, XE, 48, 128), wb=vmem(3, 2, XE, 48, 128), row_w=vmem(2, 2, 4, 16, 128), div=vmem(2, 256, 128), mixed=vmem(256, 256),
    s1=vmem(2, 256, 128), r2=vmem(2, 256, 128), s2=vmem(2, 256, 128), r3=vmem(2, 256, 128), s3=vmem(2, 256, 128),
    r4=vmem(2, 256, 128), s4=vmem(2, 256, 128), r5=vmem(2, 256, 128), lines=vmem(256, 256),
    own_out=vmem(256, 128), peer_out=vmem(256, 128),
    send_sem=DMA((4, 16)), recv_sem=DMA((4, 16)), last_send=DMA(()), last_recv=DMA(()),
)


def whole_kernel(ids_in, class_in, cond_in, first_in, forward_in, cosine_in, eigen_x_in, eigen_y_in, eigen_z_in, table_ref, normals_ref, out_ref, *scratch):
    s = dict(zip(SCRATCH, scratch))
    loads = [pltpu.make_async_copy(src, dst, s["in_sem"].at[k]) for k, (src, dst) in enumerate([
        (ids_in, s["ids"]), (class_in, s["classes"]), (cond_in, s["cond"]), (first_in, s["first"]), (forward_in, s["forward"]), (cosine_in, s["cosine"]),
        (eigen_x_in, s["eigen_x"]), (eigen_y_in, s["eigen_y"]), (eigen_z_in, s["eigen_z"])])]
    barrier = pltpu.get_barrier_semaphore()
    count = greet_halo(barrier)
    for load in loads:
        load.start()
    count += greet_groups(barrier)
    for load in loads[:3]:
        load.wait()
    fill_field(s["ids"], s["classes"], s["cond"], table_ref, s["field"], s["rows"])
    pl.semaphore_wait(barrier, count)
    copies = halo_copies(s["field"], s["rows"], s["ext"], s["row_ext"], s["halo_send"], s["halo_recv"])
    for first, _ in INNER:
        start_all(copies, ("face", first))
    start_all(copies, ("block",), "own", ("row",), ("edge",))
    for first, _ in OUTER:
        start_all(copies, ("face", first))
    for load in loads[3:]:
        load.wait()
    heat_part(normals_ref, copies, s["ext"], s["row_ext"], s["first"], s["s1"], s["root"], s["gain"], s["keep"], s["wa"], s["wb"], s["row_w"], s["div"], s["mixed"])
    solve_part(s["s1"], s["forward"], s["cosine"], s["eigen_x"], s["eigen_y"], s["eigen_z"], out_ref, s["r2"], s["s2"], s["r3"], s["s3"],
               s["r4"], s["s4"], s["r5"], s["lines"], s["own_out"], s["peer_out"], s["mixed"],
               s["send_sem"], s["recv_sem"], s["last_send"], s["last_recv"])


def per_device(surface_ids, class_map, conductivity, normals, class_table):
    cosine = cosine_table()
    eigen = eigen_values()
    cosine_pair, forward_pair = jnp.asarray(halves(cosine)), jnp.asarray(halves(cosine.T.copy()))
    along_z = np.concatenate([np.arange(0, N, 2), np.arange(1, N, 2)])
    first_pair = jnp.asarray(halves(cosine.T[along_z].copy()))
    eigen_x = jnp.asarray(np.repeat(eigen[:, None], 128, axis=1))
    eigen_y = jnp.asarray(np.repeat(eigen.reshape(16, 16), 16, axis=1))
    eigen_z = jnp.asarray(np.tile(eigen.reshape(16, 16), (1, 16)))
    out = pl.pallas_call(
        whole_kernel,
        out_shape=jax.ShapeDtypeStruct((512, 128), f32),
        in_specs=[pl.BlockSpec(memory_space=pltpu.HBM)] * 9 + [SM, VM], out_specs=VM,
        scratch_shapes=list(SCRATCH.values()),
        compiler_params=pltpu.CompilerParams(collective_id=0, has_side_effects=True, vmem_limit_bytes=LIMIT),
    )(surface_ids, class_map, conductivity, first_pair, forward_pair, cosine_pair, eigen_x, eigen_y, eigen_z, class_table, normals)
    return out.reshape(32, 16, 128)


def solution(mesh):
    spec = P("gx", "gy", "gz")
    return jax.shard_map(
        per_device, mesh=mesh, in_specs=(spec, spec, spec, P(), P()), out_specs=spec, check_vma=False
    )
```

```python
import jax
import jax.numpy as jnp
import numpy as np
from jax import lax
from jax.experimental import pallas as pl
from jax.experimental.pallas import tpu as pltpu
from jax.sharding import PartitionSpec as P

N = 256
STEPS = 8
CLASSES = 4
HALO = STEPS + 1
XE = 16 + 2 * HALO
YE = 32
time_step = 0.08
norm_floor = 0.5
f32 = jnp.float32
bf16 = jnp.bfloat16
MESH = pl.DeviceIdType.MESH


def cosine_table():
    wave_number = np.arange(N, dtype=np.float32)[:, None]
    sample = np.arange(N, dtype=np.float32)[None, :]
    factor = np.where(wave_number == 0, np.sqrt(np.float32(1.0 / N)), np.sqrt(np.float32(2.0 / N)))
    angle = np.float32(np.pi) * wave_number * (np.float32(2.0) * sample + np.float32(1.0)) / np.float32(2.0 * N)
    return (factor * np.cos(angle)).astype(np.float32)


def eigen_values():
    wave_number = np.arange(N, dtype=np.float32)
    return (np.float32(2.0) - np.float32(2.0) * np.cos(np.float32(np.pi) * wave_number / np.float32(N))).astype(np.float32)


def halves(table):
    high = table.astype(jnp.bfloat16)
    low = (table - high.astype(np.float32)).astype(jnp.bfloat16)
    return np.stack([high, low])


def split(values):
    high = values.astype(bf16)
    return high, (values - high.astype(f32)).astype(bf16)


def product(left, right):
    dot = lambda a, b: jnp.dot(a, b, preferred_element_type=f32)
    return dot(left[0], right[0]) + (dot(left[1], right[0]) + dot(left[0], right[1]))


def swap8(tile):
    row = lax.broadcasted_iota(jnp.int32, (8, 128), 0)
    group = lax.broadcasted_iota(jnp.int32, (8, 128), 1) // 16
    for bit in (1, 2, 4):
        row_bit = (row // bit) % 2
        group_bit = (group // bit) % 2
        if bit == 4:
            other = pltpu.roll(pltpu.roll(tile, 4, 0), 64, 1)
        else:
            forth = pltpu.roll(pltpu.roll(tile, bit, 0), 128 - 16 * bit, 1)
            back = pltpu.roll(pltpu.roll(tile, 8 - bit, 0), 16 * bit, 1)
            other = jnp.where(row_bit == 1, forth, back)
        tile = jnp.where(row_bit == group_bit, tile, other)
    return tile


INNER = ((7, 9), (16, 9))
OUTER = ((0, 7), (25, 7))
MARCH = True


def halo_copies(field, rows, ext, row_ext, send_sem, recv_sem):
    gx, gy, gz = lax.axis_index("gx"), lax.axis_index("gy"), lax.axis_index("gz")
    lanes = pl.ds(pl.multiple_of(gz * 128, 128), 128)
    copies = {}

    def remote(key, src, dst, x, y, core):
        slot = len(copies)
        copies[key] = pltpu.make_async_remote_copy(
            src, dst, send_sem.at[slot], recv_sem.at[slot], device_id=(x, y, core), device_id_type=MESH)

    def next_y(dy):
        return lax.rem(gy + dy + 16, 16)

    def next_x(core):
        return lax.rem(gx + 1 - 2 * core + 8, 8)

    for first, size in INNER + OUTER:
        for dy in (1, -1):
            src_rows, dst_rows = (pl.ds(8, 8), pl.ds(0, 8)) if dy == 1 else (pl.ds(0, 8), pl.ds(24, 8))
            place = ext.at[:, pl.ds(9 + first, size), dst_rows, lanes]
            remote(("face", first, dy), field.at[:, pl.ds(first, size), src_rows, :], place, gx, next_y(dy), gz)
            if (first, size) in INNER:
                remote(("pass", first, dy), place, place, gx, gy, 1 - gz)
    for dy in (1, -1):
        dst_rows = pl.ds(0, 8) if dy == 1 else pl.ds(24, 8)
        place = ext.at[:, pl.ds(9 + 25 * (1 - gz), 7), dst_rows, lanes]
        remote(("pass", "outer", dy), place, place, gx, gy, 1 - gz)
        for other in (0, 1):
            core = 1 - gz if other else gz
            remote(("corner", other, dy), ext.at[:, pl.ds(9 + 23 * (1 - core), 9), dst_rows, lanes],
                   ext.at[:, pl.ds(41 * core, 9), dst_rows, lanes], next_x(core), gy, core)
    middle_rows = pl.ds(8, 16)
    for other in (1, 0):
        core = 1 - gz if other else gz
        remote(("edge", other), field.at[:, pl.ds(23 * (1 - core), 9)], ext.at[:, pl.ds(41 * core, 9), middle_rows, lanes],
               next_x(core), gy, core)
        src, dst = field.at[:, pl.ds(7 * core, 25)], ext.at[:, pl.ds(9 + 7 * core, 25), middle_rows, lanes]
        if other:
            remote(("block", 1), src, dst, gx, gy, core)
        else:
            copies["own"] = pltpu.make_async_copy(src, dst, recv_sem.at[len(copies)])
    for side, dy in ((0, 1), (1, -1)):
        for other in (0, 1):
            core = 1 - gz if other else gz
            remote(("row", side, other), rows.at[side, :, pl.ds(pl.multiple_of(16 * core, 16), 16), :],
                   row_ext.at[side, :, :, lanes], gx, next_y(dy), core)
    return copies


def start_all(copies, *kinds):
    for kind in kinds:
        for key, copy in copies.items():
            if key == kind or key[:len(kind)] == kind:
                copy.start()


def wait_all(copies, *kinds):
    for kind in kinds:
        for key, copy in copies.items():
            if key == kind or key[:len(kind)] == kind:
                copy.wait()


def greet_halo(barrier):
    gx, gy, gz = lax.axis_index("gx"), lax.axis_index("gy"), lax.axis_index("gz")
    from_x = lax.rem(gx + 2 * gz - 1 + 8, 8)
    others = [(gx, lax.rem(gy + dy + 16, 16), core) for dy in (1, -1) for core in (0, 1)]
    others += [(gx, gy, 1 - gz), (from_x, gy, 0), (from_x, gy, 1)]
    for other in others:
        pl.semaphore_signal(barrier, inc=1, device_id=other, device_id_type=MESH)
    return len(others)


def fill_field(ids_ref, class_ref, cond_ref, table_ref, field, rows):
    lane = lax.broadcasted_iota(jnp.int32, (16, 128), 1)
    odd_first = lax.axis_index("gz")
    order = 2 * (lane % 64) + jnp.where(lane < 64, odd_first, 1 - odd_first)

    def plane(i, _):
        classes = class_ref[i]
        value = jnp.full(classes.shape, table_ref[0], f32)
        for k in range(1, CLASSES):
            value = jnp.where(classes == k, table_ref[k], value)
        root = jnp.sqrt(value * cond_ref[i])
        field[0, i] = jnp.take_along_axis(root, order, axis=1)
        field[1, i] = jnp.take_along_axis(ids_ref[i].astype(f32), order, axis=1)
        return 0
    lax.fori_loop(0, 32, plane, 0, unroll=4)
    for which in range(2):
        rows[0, which] = field[which, :, 7, :]
        rows[1, which] = field[which, :, 8, :]


def even_odd(first, second):
    low = lax.broadcasted_iota(jnp.int32, first.shape, 1) < 64
    return jnp.where(low, first, second), pltpu.roll(jnp.where(low, second, first), 64, 1)


def lookup(ids_float, tables):
    index = ids_float.astype(jnp.int32) - 1
    low = jnp.bitwise_and(index, 127)
    found = []
    for first, second in tables:
        a = jnp.take_along_axis(first, low, axis=1)
        b = jnp.take_along_axis(second, low, axis=1)
        found.append(jnp.where(index < 0, 0.0, jnp.where(index < 128, a, b)))
    return found


SWAP_UNROLL = 16
UNROLL = 6
UNALIGNED = True
LOOKUP_UNROLL = 4


def z_sides(even, odd):
    lane = lax.broadcasted_iota(jnp.int32, even.shape, 1)
    return jnp.where(lane == 0, 0.0, pltpu.roll(odd, 1, 1)), jnp.where(lane == 127, 0.0, pltpu.roll(even, 127, 1))


def z_sum(even, odd):
    before, after = z_sides(even, odd)
    return before + odd, even + after


def z_difference(even, odd):
    before, after = z_sides(even, odd)
    return odd - before, after - even


BODY = pl.ds(8, YE)


def neighbours(ref, lead, i):
    center = [ref[lead + (h, i, BODY)] for h in range(2)]
    sides = z_sum(*center)
    total = []
    for h in range(2):
        if UNALIGNED:
            y = ref[lead + (h, i, pl.ds(7, YE))] + ref[lead + (h, i, pl.ds(9, YE))]
        else:
            y = pltpu.roll(center[h], 1, 0) + pltpu.roll(center[h], YE - 1, 0)
        x = ref[lead + (h, i - 1, BODY)] + ref[lead + (h, i + 1, BODY)]
        total.append((x + y) + sides[h])
    return center, total


def heat_part(normals_ref, copies, ext, row_ext, forward_ref, out_ref, root, gain, keep, wa, wb, row_w, div, mixed):
    gx, gy, gz = lax.axis_index("gx"), lax.axis_index("gy"), lax.axis_index("gz")
    y0 = gy * 16

    def tables(r):
        return [tuple(jnp.broadcast_to(normals_ref[j:j + 1, h * 128:(h + 1) * 128], (r, 128)) for h in range(2)) for j in range(3)]

    def sources(m, parts):
        p = 33 - m + gz * (2 * m - 17)
        x = gx * 32 - HALO + p
        x_in = jnp.logical_and(x >= 0, x < N)
        done = []
        for first, count in parts:
            y = lax.broadcasted_iota(jnp.int32, (count, 128), 0) + (y0 - 8 + first)
            inside = jnp.logical_and(jnp.logical_and(y >= 0, y < N), x_in)
            both = [even_odd(*[ext[a, p, pl.ds(first, count), pl.ds(c * 128, 128)] for c in range(2)]) for a in range(2)]
            for h in range(2):
                value = jnp.where(inside, both[0][h], 0.0)
                found = lookup(both[1][h], tables(count))
                done.append((h, pl.ds(8 + first, count), value, [found[j] * value for j in range(3)]))
        for h, where, value, w in done:
            root[h, m, where] = value
            for j in range(3):
                wa[j, h, m, where] = w[j]

    def middle(m, _):
        sources(m, [(8, 16)])
        return 0

    def sides(m, _):
        sources(m, [(0, 8), (24, 8)])
        return 0

    def coefficients(m, _):
        center, total = neighbours(root, (), m)
        for h in range(2):
            keep[h, m] = 1.0 - time_step * center[h] * total[h]
            gain[h, m] = time_step * center[h] * center[h]
        return 0

    def march(src, dst, first, count):
        if not MARCH:
            for k in range(count):
                m = first + k
                done = []
                for j in range(3):
                    center, total = neighbours(src, (j,), m)
                    for h in range(2):
                        done.append((j, h, keep[h, m] * center[h] + gain[h, m] * total[h]))
                for j, h, value in done:
                    dst[j, h, m, BODY] = value
            return
        pairs = [(j, h) for j in range(3) for h in range(2)]
        for r in range(YE // 8):
            here, above, below = pl.ds(8 + 8 * r, 8), pl.ds(7 + 8 * r, 8), pl.ds(9 + 8 * r, 8)
            last = {q: src[q + (first - 1, here)] for q in pairs}
            now = {q: src[q + (first, here)] for q in pairs}
            for k in range(count):
                m = first + k
                coming = {q: src[q + (m + 1, here)] for q in pairs}
                scale = [(keep[h, m, pl.ds(8 * r, 8)], gain[h, m, pl.ds(8 * r, 8)]) for h in range(2)]
                done = {}
                for j in range(3):
                    z = z_sum(now[j, 0], now[j, 1])
                    for h in range(2):
                        q = (j, h)
                        y = src[q + (m, above)] + src[q + (m, below)]
                        done[q] = scale[h][0] * now[q] + scale[h][1] * ((last[q] + coming[q]) + (y + z[h]))
                for q in pairs:
                    dst[q + (m, here)] = done[q]
                last, now = now, coming

    def unit(m, _):
        for h in range(2):
            w = [wa[j, h, m, BODY] for j in range(3)]
            size = jnp.sqrt(w[0] * w[0] + w[1] * w[1] + w[2] * w[2])
            floor = jnp.maximum(jnp.maximum(size, norm_floor * root[h, m, BODY]), 1e-30)
            scale = 0.5 / floor
            for j in range(3):
                wb[j, h, m, BODY] = w[j] * scale
        return 0

    def looked_up(body, first, end):
        lax.fori_loop(first, end, body, 0, unroll=LOOKUP_UNROLL)

    zero = jnp.zeros((XE, 128), f32)
    for row in (7, 40):
        for h in range(2):
            root[h, :, row, :] = zero
            for j in range(3):
                wa[j, h, :, row, :] = zero
                wb[j, h, :, row, :] = zero

    wait_all(copies, "own", ("block",))
    looked_up(middle, 0, 12)
    for first, _ in INNER:
        for dy in (1, -1):
            copies["face", first, dy].wait()
            copies["pass", first, dy].start()
    for first, _ in OUTER:
        start_all(copies, ("face", first))
    looked_up(middle, 12, 25)
    wait_all(copies, ("edge",))
    looked_up(middle, 25, XE)
    wait_all(copies, ("row",))
    for side in range(2):
        y = y0 - 9 if side == 0 else y0 + 24
        y_in = jnp.logical_and(y >= 0, y < N)
        both = [even_odd(*[row_ext[side, a, :, pl.ds(c * 128, 128)] for c in range(2)]) for a in range(2)]
        for h in range(2):
            value = jnp.where(y_in, both[0][h], 0.0)
            found = lookup(both[1][h], tables(16))
            row_w[side, h, 3] = value
            for j in range(3):
                row_w[side, h, j] = found[j] * value

    def outer_row(m, _):
        k = 24 - m + gz * (2 * m - 33)
        for side, row in ((0, 7), (1, 40)):
            for h in range(2):
                root[h, m, pl.ds(row, 1)] = row_w[side, h, 3, pl.ds(k, 1)]
                for j in range(3):
                    wa[j, h, m, pl.ds(row, 1)] = row_w[side, h, j, pl.ds(k, 1)]
        return 0
    lax.fori_loop(9, 25, outer_row, 0, unroll=4)

    for before, reach in ((0, 18), (18, 25), (25, XE)):
        if before == 0:
            wait_all(copies, ("pass", INNER[0][0]), ("pass", INNER[1][0]))
        elif before == 18:
            wait_all(copies, ("pass", "outer"))
        else:
            wait_all(copies, ("corner",))
        looked_up(sides, before, reach)
        lax.fori_loop(max(1, before - 1), reach - 1, coefficients, 0, unroll=UNROLL)
        if before == 0:
            for first, _ in OUTER:
                for dy in (1, -1):
                    copies["face", first, dy].wait()
            start_all(copies, ("pass", "outer"), ("corner",))
            for step in range(1, STEPS + 1):
                src, dst = (wa, wb) if step % 2 else (wb, wa)
                march(src, dst, step, reach - 2 * step)
        else:
            def pair(p, _, before=before, reach=reach):
                for odd, src, dst in ((1, wa, wb), (2, wb, wa)):
                    march(src, dst, before - odd - 2 * p, reach - before)
                return 0
            lax.fori_loop(0, STEPS // 2, pair, 0)
        first = max(STEPS, before - STEPS - 1)
        end = XE - STEPS if reach == XE else reach - STEPS - 1
        lax.fori_loop(first, end, unit, 0, unroll=min(UNROLL, end - first))

    sign = (2 * gz - 1).astype(f32)

    def divergence(k, _):
        m = 24 - k + gz * (2 * k - 15)
        part_z = z_difference(*[wb[2, h, m, pl.ds(16, 16)] for h in range(2)])
        for h in range(2):
            part_x = sign * (wb[0, h, m + 1, pl.ds(16, 16)] - wb[0, h, m - 1, pl.ds(16, 16)])
            part_y = wb[1, h, m, pl.ds(17, 16)] - wb[1, h, m, pl.ds(15, 16)]
            div[h, pl.ds(pl.multiple_of(k * 16, 16), 16), :] = part_x + part_y + part_z[h]
        return 0
    lax.fori_loop(0, 16, divergence, 0, unroll=4)

    lines = jnp.concatenate(
        [jnp.concatenate([div[h, pl.ds(y, 16, stride=16), :] for y in range(16)], axis=0) for h in range(2)], axis=1)
    mixed[...] = product(split(lines), (forward_ref[0], forward_ref[1]))

    def spread(y, _):
        for xh in range(2):
            for ah in range(2):
                tile = mixed[pl.ds(pl.multiple_of(y * 16 + xh * 8, 8), 8), pl.ds(ah * 128, 128)]
                out_ref[xh, pl.ds(ah * 128 + y, 8, stride=16), :] = swap8(tile)
        return 0
    lax.fori_loop(0, 16, spread, 0, unroll=SWAP_UNROLL)


def y_group(index):
    return (lax.axis_index("gx"), index, lax.axis_index("gz"))


def x_group(index):
    return (index // 2, lax.axis_index("gy"), index % 2)


FAR_FIRST_Y = (4, 12, 5, 11, 3, 13, 6, 10, 2, 14, 7, 9, 1, 15, 8)
FAR_FIRST_X = (12, 4, 11, 13, 3, 5, 10, 14, 2, 6, 8, 7, 9, 1, 15)


def exchange(src, dst, me, where, order, send_sem, recv_sem):
    def copy(d):
        to = lax.rem(me + d, 16)
        return pltpu.make_async_remote_copy(
            src.at[:, pl.ds(pl.multiple_of(to * 16, 16), 16), :],
            dst.at[:, pl.ds(pl.multiple_of(me * 16, 16), 16), :],
            send_sem.at[d], recv_sem.at[d], device_id=where(to), device_id_type=MESH)

    for d in order:
        copy(d).start()
    own = pl.ds(pl.multiple_of(me * 16, 16), 16)
    dst[:, own, :] = src[:, own, :]

    for d in range(1, 16):
        copy(d).wait()


def whole(ref):
    return jnp.concatenate([ref[0], ref[1]], axis=1)


def turn(values, mixed, dst):
    mixed[...] = values

    def block(b, _):
        for rh in range(2):
            for gh in range(2):
                tile = mixed[pl.ds(pl.multiple_of(b * 16 + rh * 8, 8), 8), pl.ds(gh * 128, 128)]
                dst[rh, pl.ds(pl.multiple_of(b * 16 + gh * 8, 8), 8), :] = swap8(tile)
        return 0
    lax.fori_loop(0, 16, block, 0, unroll=SWAP_UNROLL)


def greet_groups(barrier):
    gx, gy, gz = lax.axis_index("gx"), lax.axis_index("gy"), lax.axis_index("gz")
    group = gx * 2 + gz

    for dy, dx in zip(FAR_FIRST_Y, FAR_FIRST_X):
        pl.semaphore_signal(barrier, inc=1, device_id=y_group(lax.rem(gy + dy, 16)), device_id_type=MESH)
        pl.semaphore_signal(barrier, inc=1, device_id=x_group(lax.rem(group + dx, 16)), device_id_type=MESH)
    return 30


def solve_part(s1, forward_ref, cosine_ref, eigen_x, eigen_y, eigen_z, out_ref, r2, s2, r3, s3, r4, s4, r5, lines, own_out, peer_out, mixed,
               send_sem, recv_sem, last_send, last_recv):
    gx, gy, gz = lax.axis_index("gx"), lax.axis_index("gy"), lax.axis_index("gz")
    group = gx * 2 + gz
    cosine = (cosine_ref[0], cosine_ref[1])
    forward = (forward_ref[0], forward_ref[1])
    exchange(s1, r2, gy, y_group, FAR_FIRST_Y, send_sem.at[0], recv_sem.at[0])
    turn(product(cosine, split(whole(r2))), mixed, s2)
    exchange(s2, r3, group, x_group, FAR_FIRST_X, send_sem.at[1], recv_sem.at[1])
    spectrum = product(cosine, split(whole(r3)))
    rest = eigen_y[pl.ds(group, 1), :] + eigen_z[pl.ds(gy, 1), :]
    eigen = jnp.concatenate([eigen_x[...], eigen_x[...]], axis=1)
    solved = -spectrum / (eigen + rest + 4.0 / (N * N))
    turn(product(forward, split(solved)), mixed, s3)
    exchange(s3, r4, group, x_group, FAR_FIRST_X, send_sem.at[2], recv_sem.at[2])
    values = product(forward, split(whole(r4)))
    for h in range(2):
        s4[h] = values[:, h * 128:(h + 1) * 128]
    exchange(s4, r5, gy, y_group, FAR_FIRST_Y, send_sem.at[3], recv_sem.at[3])

    def gather(y, _):
        for xh in range(2):
            for ah in range(2):
                tile = r5[xh, pl.ds(ah * 128 + y, 8, stride=16), :]
                lines[pl.ds(pl.multiple_of(y * 16 + xh * 8, 8), 8), pl.ds(ah * 128, 128)] = swap8(tile)
        return 0
    lax.fori_loop(0, 16, gather, 0, unroll=SWAP_UNROLL)
    pieces = split(lines[...])

    def half_of(core):
        lanes = pl.ds(pl.multiple_of(core * 128, 128), 128)
        return product(pieces, (cosine_ref[0, :, lanes], cosine_ref[1, :, lanes]))

    theirs = half_of(1 - gz)
    for y in range(16):
        peer_out[pl.ds(y, 16, stride=16), :] = theirs[y * 16:(y + 1) * 16]
    rows = pl.ds(pl.multiple_of(gz * 256, 256), 256)
    copy = pltpu.make_async_remote_copy(
        peer_out, out_ref.at[rows, :], last_send, last_recv, device_id=(gx, gy, 1 - gz), device_id_type=MESH)
    copy.start()
    mine = half_of(gz)
    for y in range(16):
        own_out[pl.ds(y, 16, stride=16), :] = mine[y * 16:(y + 1) * 16]
    out_ref[rows, :] = own_out[...]
    copy.wait()


VM = pl.BlockSpec(memory_space=pltpu.VMEM)
SM = pl.BlockSpec(memory_space=pltpu.SMEM)
DMA = pltpu.SemaphoreType.DMA
LIMIT = 62 * 1024 * 1024


def vmem(*shape):
    return pltpu.VMEM(shape, f32)


SCRATCH = dict(
    ids=pltpu.VMEM((32, 16, 128), jnp.int32), classes=pltpu.VMEM((32, 16, 128), jnp.int32), cond=vmem(32, 16, 128),
    first=pltpu.VMEM((2, 256, 256), bf16), forward=pltpu.VMEM((2, 256, 256), bf16), cosine=pltpu.VMEM((2, 256, 256), bf16),
    eigen_x=vmem(256, 128), eigen_y=vmem(16, 256), eigen_z=vmem(16, 256), in_sem=DMA((9,)),
    field=vmem(2, 32, 16, 128), rows=vmem(2, 2, 32, 128), ext=vmem(2, 50, YE, 256), row_ext=vmem(2, 2, 16, 256),
    halo_send=DMA((40,)), halo_recv=DMA((40,)),
    root=vmem(2, XE, 48, 128), gain=vmem(2, XE, YE, 128), keep=vmem(2, XE, YE, 128),
    wa=vmem(3, 2, XE, 48, 128), wb=vmem(3, 2, XE, 48, 128), row_w=vmem(2, 2, 4, 16, 128), div=vmem(2, 256, 128), mixed=vmem(256, 256),
    s1=vmem(2, 256, 128), r2=vmem(2, 256, 128), s2=vmem(2, 256, 128), r3=vmem(2, 256, 128), s3=vmem(2, 256, 128),
    r4=vmem(2, 256, 128), s4=vmem(2, 256, 128), r5=vmem(2, 256, 128), lines=vmem(256, 256),
    own_out=vmem(256, 128), peer_out=vmem(256, 128),
    send_sem=DMA((4, 16)), recv_sem=DMA((4, 16)), last_send=DMA(()), last_recv=DMA(()),
)


def whole_kernel(ids_in, class_in, cond_in, first_in, forward_in, cosine_in, eigen_x_in, eigen_y_in, eigen_z_in, table_ref, normals_ref, out_ref, *scratch):
    s = dict(zip(SCRATCH, scratch))
    loads = [pltpu.make_async_copy(src, dst, s["in_sem"].at[k]) for k, (src, dst) in enumerate([
        (ids_in, s["ids"]), (class_in, s["classes"]), (cond_in, s["cond"]), (first_in, s["first"]), (forward_in, s["forward"]), (cosine_in, s["cosine"]),
        (eigen_x_in, s["eigen_x"]), (eigen_y_in, s["eigen_y"]), (eigen_z_in, s["eigen_z"])])]
    barrier = pltpu.get_barrier_semaphore()
    for load in loads[:3]:
        load.start()
    count = greet_groups(barrier) + greet_halo(barrier)
    for load in loads[3:]:
        load.start()
    for load in loads[:3]:
        load.wait()
    fill_field(s["ids"], s["classes"], s["cond"], table_ref, s["field"], s["rows"])
    pl.semaphore_wait(barrier, count)
    copies = halo_copies(s["field"], s["rows"], s["ext"], s["row_ext"], s["halo_send"], s["halo_recv"])
    for first, _ in INNER:
        start_all(copies, ("face", first))
    start_all(copies, "own", ("block",), ("row",), ("edge",))
    for load in loads[3:]:
        load.wait()
    heat_part(normals_ref, copies, s["ext"], s["row_ext"], s["first"], s["s1"], s["root"], s["gain"], s["keep"], s["wa"], s["wb"], s["row_w"], s["div"], s["mixed"])
    solve_part(s["s1"], s["forward"], s["cosine"], s["eigen_x"], s["eigen_y"], s["eigen_z"], out_ref, s["r2"], s["s2"], s["r3"], s["s3"],
               s["r4"], s["s4"], s["r5"], s["lines"], s["own_out"], s["peer_out"], s["mixed"],
               s["send_sem"], s["recv_sem"], s["last_send"], s["last_recv"])


def per_device(surface_ids, class_map, conductivity, normals, class_table):
    cosine = cosine_table()
    eigen = eigen_values()
    cosine_pair, forward_pair = jnp.asarray(halves(cosine)), jnp.asarray(halves(cosine.T.copy()))
    along_z = np.concatenate([np.arange(0, N, 2), np.arange(1, N, 2)])
    first_pair = jnp.asarray(halves(cosine.T[along_z].copy()))
    eigen_x = jnp.asarray(np.repeat(eigen[:, None], 128, axis=1))
    eigen_y = jnp.asarray(np.repeat(eigen.reshape(16, 16), 16, axis=1))
    eigen_z = jnp.asarray(np.tile(eigen.reshape(16, 16), (1, 16)))
    out = pl.pallas_call(
        whole_kernel,
        out_shape=jax.ShapeDtypeStruct((512, 128), f32),
        in_specs=[pl.BlockSpec(memory_space=pltpu.HBM)] * 9 + [SM, VM], out_specs=VM,
        scratch_shapes=list(SCRATCH.values()),
        compiler_params=pltpu.CompilerParams(collective_id=0, has_side_effects=True, vmem_limit_bytes=LIMIT),
    )(surface_ids, class_map, conductivity, first_pair, forward_pair, cosine_pair, eigen_x, eigen_y, eigen_z, class_table, normals)
    return out.reshape(32, 16, 128)


def solution(mesh):
    spec = P("gx", "gy", "gz")
    return jax.shard_map(
        per_device, mesh=mesh, in_specs=(spec, spec, spec, P(), P()), out_specs=spec, check_vma=False
    )
```

```python
import jax
import jax.numpy as jnp
import numpy as np
from jax import lax
from jax.experimental import pallas as pl
from jax.experimental.pallas import tpu as pltpu
from jax.sharding import PartitionSpec as P

N = 256
STEPS = 8
CLASSES = 4
HALO = STEPS + 1
XE = 16 + 2 * HALO
YE = 32
time_step = 0.08
norm_floor = 0.5
f32 = jnp.float32
bf16 = jnp.bfloat16
MESH = pl.DeviceIdType.MESH


def cosine_table():
    wave_number = np.arange(N, dtype=np.float32)[:, None]
    sample = np.arange(N, dtype=np.float32)[None, :]
    factor = np.where(wave_number == 0, np.sqrt(np.float32(1.0 / N)), np.sqrt(np.float32(2.0 / N)))
    angle = np.float32(np.pi) * wave_number * (np.float32(2.0) * sample + np.float32(1.0)) / np.float32(2.0 * N)
    return (factor * np.cos(angle)).astype(np.float32)


def eigen_values():
    wave_number = np.arange(N, dtype=np.float32)
    return (np.float32(2.0) - np.float32(2.0) * np.cos(np.float32(np.pi) * wave_number / np.float32(N))).astype(np.float32)


def halves(table):
    high = table.astype(jnp.bfloat16)
    low = (table - high.astype(np.float32)).astype(jnp.bfloat16)
    return np.stack([high, low])


def split(values):
    high = values.astype(bf16)
    return high, (values - high.astype(f32)).astype(bf16)


def product(left, right):
    dot = lambda a, b: jnp.dot(a, b, preferred_element_type=f32)
    return dot(left[0], right[0]) + (dot(left[1], right[0]) + dot(left[0], right[1]))


def swap8(tile):
    row = lax.broadcasted_iota(jnp.int32, (8, 128), 0)
    group = lax.broadcasted_iota(jnp.int32, (8, 128), 1) // 16
    for bit in (1, 2, 4):
        row_bit = (row // bit) % 2
        group_bit = (group // bit) % 2
        if bit == 4:
            other = pltpu.roll(pltpu.roll(tile, 4, 0), 64, 1)
        else:
            forth = pltpu.roll(pltpu.roll(tile, bit, 0), 128 - 16 * bit, 1)
            back = pltpu.roll(pltpu.roll(tile, 8 - bit, 0), 16 * bit, 1)
            other = jnp.where(row_bit == 1, forth, back)
        tile = jnp.where(row_bit == group_bit, tile, other)
    return tile


INNER = ((7, 9), (16, 9))
OUTER = ((0, 7), (25, 7))
MARCH = True


def halo_copies(field, rows, ext, row_ext, send_sem, recv_sem):
    gx, gy, gz = lax.axis_index("gx"), lax.axis_index("gy"), lax.axis_index("gz")
    lanes = pl.ds(pl.multiple_of(gz * 128, 128), 128)
    copies = {}

    def remote(key, src, dst, x, y, core):
        slot = len(copies)
        copies[key] = pltpu.make_async_remote_copy(
            src, dst, send_sem.at[slot], recv_sem.at[slot], device_id=(x, y, core), device_id_type=MESH)

    def next_y(dy):
        return lax.rem(gy + dy + 16, 16)

    def next_x(core):
        return lax.rem(gx + 1 - 2 * core + 8, 8)

    for first, size in INNER + OUTER:
        for dy in (1, -1):
            src_rows, dst_rows = (pl.ds(8, 8), pl.ds(0, 8)) if dy == 1 else (pl.ds(0, 8), pl.ds(24, 8))
            place = ext.at[:, pl.ds(9 + first, size), dst_rows, lanes]
            remote(("face", first, dy), field.at[:, pl.ds(first, size), src_rows, :], place, gx, next_y(dy), gz)
            if (first, size) in INNER:
                remote(("pass", first, dy), place, place, gx, gy, 1 - gz)
    for dy in (1, -1):
        dst_rows = pl.ds(0, 8) if dy == 1 else pl.ds(24, 8)
        place = ext.at[:, pl.ds(9 + 25 * (1 - gz), 7), dst_rows, lanes]
        remote(("pass", "outer", dy), place, place, gx, gy, 1 - gz)
        for other in (0, 1):
            core = 1 - gz if other else gz
            remote(("corner", other, dy), ext.at[:, pl.ds(9 + 23 * (1 - core), 9), dst_rows, lanes],
                   ext.at[:, pl.ds(41 * core, 9), dst_rows, lanes], next_x(core), gy, core)
    middle_rows = pl.ds(8, 16)
    for other in (1, 0):
        core = 1 - gz if other else gz
        remote(("edge", other), field.at[:, pl.ds(23 * (1 - core), 9)], ext.at[:, pl.ds(41 * core, 9), middle_rows, lanes],
               next_x(core), gy, core)
        src, dst = field.at[:, pl.ds(7 * core, 25)], ext.at[:, pl.ds(9 + 7 * core, 25), middle_rows, lanes]
        if other:
            remote(("block", 1), src, dst, gx, gy, core)
        else:
            copies["own"] = pltpu.make_async_copy(src, dst, recv_sem.at[len(copies)])
    for side, dy in ((0, 1), (1, -1)):
        for other in (0, 1):
            core = 1 - gz if other else gz
            remote(("row", side, other), rows.at[side, :, pl.ds(pl.multiple_of(16 * core, 16), 16), :],
                   row_ext.at[side, :, :, lanes], gx, next_y(dy), core)
    return copies


def start_all(copies, *kinds):
    for kind in kinds:
        for key, copy in copies.items():
            if key == kind or key[:len(kind)] == kind:
                copy.start()


def wait_all(copies, *kinds):
    for kind in kinds:
        for key, copy in copies.items():
            if key == kind or key[:len(kind)] == kind:
                copy.wait()


def greet_halo(barrier):
    gx, gy, gz = lax.axis_index("gx"), lax.axis_index("gy"), lax.axis_index("gz")
    from_x = lax.rem(gx + 2 * gz - 1 + 8, 8)
    others = [(gx, lax.rem(gy + dy + 16, 16), core) for dy in (1, -1) for core in (0, 1)]
    others += [(gx, gy, 1 - gz), (from_x, gy, 0), (from_x, gy, 1)]
    for other in others:
        pl.semaphore_signal(barrier, inc=1, device_id=other, device_id_type=MESH)
    return len(others)


def fill_field(ids_ref, class_ref, cond_ref, table_ref, field, rows):
    lane = lax.broadcasted_iota(jnp.int32, (16, 128), 1)
    odd_first = lax.axis_index("gz")
    order = 2 * (lane % 64) + jnp.where(lane < 64, odd_first, 1 - odd_first)

    def plane(i, _):
        classes = class_ref[i]
        value = jnp.full(classes.shape, table_ref[0], f32)
        for k in range(1, CLASSES):
            value = jnp.where(classes == k, table_ref[k], value)
        root = jnp.sqrt(value * cond_ref[i])
        field[0, i] = jnp.take_along_axis(root, order, axis=1)
        field[1, i] = jnp.take_along_axis(ids_ref[i].astype(f32), order, axis=1)
        return 0
    lax.fori_loop(0, 32, plane, 0, unroll=4)
    for which in range(2):
        rows[0, which] = field[which, :, 7, :]
        rows[1, which] = field[which, :, 8, :]


def even_odd(first, second):
    low = lax.broadcasted_iota(jnp.int32, first.shape, 1) < 64
    return jnp.where(low, first, second), pltpu.roll(jnp.where(low, second, first), 64, 1)


def lookup(ids_float, tables):
    index = ids_float.astype(jnp.int32) - 1
    low = jnp.bitwise_and(index, 127)
    found = []
    for first, second in tables:
        a = jnp.take_along_axis(first, low, axis=1)
        b = jnp.take_along_axis(second, low, axis=1)
        found.append(jnp.where(index < 0, 0.0, jnp.where(index < 128, a, b)))
    return found


SWAP_UNROLL = 16
UNROLL = 6
UNALIGNED = True
LOOKUP_UNROLL = 4


def z_sides(even, odd):
    lane = lax.broadcasted_iota(jnp.int32, even.shape, 1)
    return jnp.where(lane == 0, 0.0, pltpu.roll(odd, 1, 1)), jnp.where(lane == 127, 0.0, pltpu.roll(even, 127, 1))


def z_sum(even, odd):
    before, after = z_sides(even, odd)
    return before + odd, even + after


def z_difference(even, odd):
    before, after = z_sides(even, odd)
    return odd - before, after - even


BODY = pl.ds(8, YE)


def neighbours(ref, lead, i):
    center = [ref[lead + (h, i, BODY)] for h in range(2)]
    sides = z_sum(*center)
    total = []
    for h in range(2):
        if UNALIGNED:
            y = ref[lead + (h, i, pl.ds(7, YE))] + ref[lead + (h, i, pl.ds(9, YE))]
        else:
            y = pltpu.roll(center[h], 1, 0) + pltpu.roll(center[h], YE - 1, 0)
        x = ref[lead + (h, i - 1, BODY)] + ref[lead + (h, i + 1, BODY)]
        total.append((x + y) + sides[h])
    return center, total


def heat_part(normals_ref, copies, ext, row_ext, forward_ref, out_ref, root, gain, keep, wa, wb, row_w, div, mixed):
    gx, gy, gz = lax.axis_index("gx"), lax.axis_index("gy"), lax.axis_index("gz")
    y0 = gy * 16

    def tables(r):
        return [tuple(jnp.broadcast_to(normals_ref[j:j + 1, h * 128:(h + 1) * 128], (r, 128)) for h in range(2)) for j in range(3)]

    def sources(m, parts):
        p = 33 - m + gz * (2 * m - 17)
        x = gx * 32 - HALO + p
        x_in = jnp.logical_and(x >= 0, x < N)
        done = []
        for first, count in parts:
            y = lax.broadcasted_iota(jnp.int32, (count, 128), 0) + (y0 - 8 + first)
            inside = jnp.logical_and(jnp.logical_and(y >= 0, y < N), x_in)
            both = [even_odd(*[ext[a, p, pl.ds(first, count), pl.ds(c * 128, 128)] for c in range(2)]) for a in range(2)]
            for h in range(2):
                value = jnp.where(inside, both[0][h], 0.0)
                found = lookup(both[1][h], tables(count))
                done.append((h, pl.ds(8 + first, count), value, [found[j] * value for j in range(3)]))
        for h, where, value, w in done:
            root[h, m, where] = value
            for j in range(3):
                wa[j, h, m, where] = w[j]

    def middle(m, _):
        sources(m, [(8, 16)])
        return 0

    def sides(m, _):
        sources(m, [(0, 8), (24, 8)])
        return 0

    def coefficients(m, _):
        center, total = neighbours(root, (), m)
        for h in range(2):
            keep[h, m] = 1.0 - time_step * center[h] * total[h]
            gain[h, m] = time_step * center[h] * center[h]
        return 0

    def march(src, dst, first, count):
        if not MARCH:
            for k in range(count):
                m = first + k
                done = []
                for j in range(3):
                    center, total = neighbours(src, (j,), m)
                    for h in range(2):
                        done.append((j, h, keep[h, m] * center[h] + gain[h, m] * total[h]))
                for j, h, value in done:
                    dst[j, h, m, BODY] = value
            return
        pairs = [(j, h) for j in range(3) for h in range(2)]
        for r in range(YE // 8):
            here, above, below = pl.ds(8 + 8 * r, 8), pl.ds(7 + 8 * r, 8), pl.ds(9 + 8 * r, 8)
            last = {q: src[q + (first - 1, here)] for q in pairs}
            now = {q: src[q + (first, here)] for q in pairs}
            for k in range(count):
                m = first + k
                coming = {q: src[q + (m + 1, here)] for q in pairs}
                scale = [(keep[h, m, pl.ds(8 * r, 8)], gain[h, m, pl.ds(8 * r, 8)]) for h in range(2)]
                done = {}
                for j in range(3):
                    z = z_sum(now[j, 0], now[j, 1])
                    for h in range(2):
                        q = (j, h)
                        y = src[q + (m, above)] + src[q + (m, below)]
                        done[q] = scale[h][0] * now[q] + scale[h][1] * ((last[q] + coming[q]) + (y + z[h]))
                for q in pairs:
                    dst[q + (m, here)] = done[q]
                last, now = now, coming

    def unit(m, _):
        for h in range(2):
            w = [wa[j, h, m, BODY] for j in range(3)]
            size = jnp.sqrt(w[0] * w[0] + w[1] * w[1] + w[2] * w[2])
            floor = jnp.maximum(jnp.maximum(size, norm_floor * root[h, m, BODY]), 1e-30)
            scale = 0.5 / floor
            for j in range(3):
                wb[j, h, m, BODY] = w[j] * scale
        return 0

    def looked_up(body, first, end):
        lax.fori_loop(first, end, body, 0, unroll=LOOKUP_UNROLL)

    zero = jnp.zeros((XE, 128), f32)
    for row in (7, 40):
        for h in range(2):
            root[h, :, row, :] = zero
            for j in range(3):
                wa[j, h, :, row, :] = zero
                wb[j, h, :, row, :] = zero

    wait_all(copies, "own", ("block",))
    looked_up(middle, 0, 12)
    for first, _ in INNER:
        for dy in (1, -1):
            copies["face", first, dy].wait()
            copies["pass", first, dy].start()
    for first, _ in OUTER:
        start_all(copies, ("face", first))
    looked_up(middle, 12, 25)
    wait_all(copies, ("edge",))
    looked_up(middle, 25, XE)
    wait_all(copies, ("row",))
    for side in range(2):
        y = y0 - 9 if side == 0 else y0 + 24
        y_in = jnp.logical_and(y >= 0, y < N)
        both = [even_odd(*[row_ext[side, a, :, pl.ds(c * 128, 128)] for c in range(2)]) for a in range(2)]
        for h in range(2):
            value = jnp.where(y_in, both[0][h], 0.0)
            found = lookup(both[1][h], tables(16))
            row_w[side, h, 3] = value
            for j in range(3):
                row_w[side, h, j] = found[j] * value

    def outer_row(m, _):
        k = 24 - m + gz * (2 * m - 33)
        for side, row in ((0, 7), (1, 40)):
            for h in range(2):
                root[h, m, pl.ds(row, 1)] = row_w[side, h, 3, pl.ds(k, 1)]
                for j in range(3):
                    wa[j, h, m, pl.ds(row, 1)] = row_w[side, h, j, pl.ds(k, 1)]
        return 0
    lax.fori_loop(9, 25, outer_row, 0, unroll=4)

    for before, reach in ((0, 18), (18, 25), (25, XE)):
        if before == 0:
            wait_all(copies, ("pass", INNER[0][0]), ("pass", INNER[1][0]))
        elif before == 18:
            wait_all(copies, ("pass", "outer"))
        else:
            wait_all(copies, ("corner",))
        looked_up(sides, before, reach)
        lax.fori_loop(max(1, before - 1), reach - 1, coefficients, 0, unroll=UNROLL)
        if before == 0:
            for step in range(1, STEPS + 1):
                src, dst = (wa, wb) if step % 2 else (wb, wa)
                march(src, dst, step, reach - 2 * step)
                if step == 2:
                    for first, _ in OUTER:
                        for dy in (1, -1):
                            copies["face", first, dy].wait()
                    start_all(copies, ("pass", "outer"), ("corner",))
        else:
            def pair(p, _, before=before, reach=reach):
                for odd, src, dst in ((1, wa, wb), (2, wb, wa)):
                    march(src, dst, before - odd - 2 * p, reach - before)
                return 0
            lax.fori_loop(0, STEPS // 2, pair, 0)
        first = max(STEPS, before - STEPS - 1)
        end = XE - STEPS if reach == XE else reach - STEPS - 1
        lax.fori_loop(first, end, unit, 0, unroll=min(UNROLL, end - first))

    sign = (2 * gz - 1).astype(f32)

    def divergence(k, _):
        m = 24 - k + gz * (2 * k - 15)
        part_z = z_difference(*[wb[2, h, m, pl.ds(16, 16)] for h in range(2)])
        for h in range(2):
            part_x = sign * (wb[0, h, m + 1, pl.ds(16, 16)] - wb[0, h, m - 1, pl.ds(16, 16)])
            part_y = wb[1, h, m, pl.ds(17, 16)] - wb[1, h, m, pl.ds(15, 16)]
            div[h, pl.ds(pl.multiple_of(k * 16, 16), 16), :] = part_x + part_y + part_z[h]
        return 0
    lax.fori_loop(0, 16, divergence, 0, unroll=4)

    lines = jnp.concatenate(
        [jnp.concatenate([div[h, pl.ds(y, 16, stride=16), :] for y in range(16)], axis=0) for h in range(2)], axis=1)
    mixed[...] = product(split(lines), (forward_ref[0], forward_ref[1]))

    def spread(y, _):
        for xh in range(2):
            for ah in range(2):
                tile = mixed[pl.ds(pl.multiple_of(y * 16 + xh * 8, 8), 8), pl.ds(ah * 128, 128)]
                out_ref[xh, pl.ds(ah * 128 + y, 8, stride=16), :] = swap8(tile)
        return 0
    lax.fori_loop(0, 16, spread, 0, unroll=SWAP_UNROLL)


def y_group(index):
    return (lax.axis_index("gx"), index, lax.axis_index("gz"))


def x_group(index):
    return (index // 2, lax.axis_index("gy"), index % 2)


FAR_FIRST_Y = (4, 12, 5, 11, 3, 13, 6, 10, 2, 14, 7, 9, 1, 15, 8)
FAR_FIRST_X = (12, 4, 11, 13, 3, 5, 10, 14, 2, 6, 8, 7, 9, 1, 15)


def exchange(src, dst, me, where, order, send_sem, recv_sem):
    def copy(d):
        to = lax.rem(me + d, 16)
        return pltpu.make_async_remote_copy(
            src.at[:, pl.ds(pl.multiple_of(to * 16, 16), 16), :],
            dst.at[:, pl.ds(pl.multiple_of(me * 16, 16), 16), :],
            send_sem.at[d], recv_sem.at[d], device_id=where(to), device_id_type=MESH)

    for d in order:
        copy(d).start()
    own = pl.ds(pl.multiple_of(me * 16, 16), 16)
    dst[:, own, :] = src[:, own, :]

    for d in range(1, 16):
        copy(d).wait()


def whole(ref):
    return jnp.concatenate([ref[0], ref[1]], axis=1)


def turn(values, mixed, dst):
    mixed[...] = values

    def block(b, _):
        for rh in range(2):
            for gh in range(2):
                tile = mixed[pl.ds(pl.multiple_of(b * 16 + rh * 8, 8), 8), pl.ds(gh * 128, 128)]
                dst[rh, pl.ds(pl.multiple_of(b * 16 + gh * 8, 8), 8), :] = swap8(tile)
        return 0
    lax.fori_loop(0, 16, block, 0, unroll=SWAP_UNROLL)


def greet_groups(barrier):
    gx, gy, gz = lax.axis_index("gx"), lax.axis_index("gy"), lax.axis_index("gz")
    group = gx * 2 + gz

    for dy, dx in zip(FAR_FIRST_Y, FAR_FIRST_X):
        pl.semaphore_signal(barrier, inc=1, device_id=y_group(lax.rem(gy + dy, 16)), device_id_type=MESH)
        pl.semaphore_signal(barrier, inc=1, device_id=x_group(lax.rem(group + dx, 16)), device_id_type=MESH)
    return 30


def solve_part(s1, forward_ref, cosine_ref, eigen_x, eigen_y, eigen_z, out_ref, r2, s2, r3, s3, r4, s4, r5, lines, own_out, peer_out, mixed,
               send_sem, recv_sem, last_send, last_recv):
    gx, gy, gz = lax.axis_index("gx"), lax.axis_index("gy"), lax.axis_index("gz")
    group = gx * 2 + gz
    cosine = (cosine_ref[0], cosine_ref[1])
    forward = (forward_ref[0], forward_ref[1])
    exchange(s1, r2, gy, y_group, FAR_FIRST_Y, send_sem.at[0], recv_sem.at[0])
    turn(product(cosine, split(whole(r2))), mixed, s2)
    exchange(s2, r3, group, x_group, FAR_FIRST_X, send_sem.at[1], recv_sem.at[1])
    spectrum = product(cosine, split(whole(r3)))
    rest = eigen_y[pl.ds(group, 1), :] + eigen_z[pl.ds(gy, 1), :]
    eigen = jnp.concatenate([eigen_x[...], eigen_x[...]], axis=1)
    solved = -spectrum / (eigen + rest + 4.0 / (N * N))
    turn(product(forward, split(solved)), mixed, s3)
    exchange(s3, r4, group, x_group, FAR_FIRST_X, send_sem.at[2], recv_sem.at[2])
    values = product(forward, split(whole(r4)))
    for h in range(2):
        s4[h] = values[:, h * 128:(h + 1) * 128]
    exchange(s4, r5, gy, y_group, FAR_FIRST_Y, send_sem.at[3], recv_sem.at[3])

    def gather(y, _):
        for xh in range(2):
            for ah in range(2):
                tile = r5[xh, pl.ds(ah * 128 + y, 8, stride=16), :]
                lines[pl.ds(pl.multiple_of(y * 16 + xh * 8, 8), 8), pl.ds(ah * 128, 128)] = swap8(tile)
        return 0
    lax.fori_loop(0, 16, gather, 0, unroll=SWAP_UNROLL)
    pieces = split(lines[...])

    def half_of(core):
        lanes = pl.ds(pl.multiple_of(core * 128, 128), 128)
        return product(pieces, (cosine_ref[0, :, lanes], cosine_ref[1, :, lanes]))

    theirs = half_of(1 - gz)
    for y in range(16):
        peer_out[pl.ds(y, 16, stride=16), :] = theirs[y * 16:(y + 1) * 16]
    rows = pl.ds(pl.multiple_of(gz * 256, 256), 256)
    copy = pltpu.make_async_remote_copy(
        peer_out, out_ref.at[rows, :], last_send, last_recv, device_id=(gx, gy, 1 - gz), device_id_type=MESH)
    copy.start()
    mine = half_of(gz)
    for y in range(16):
        own_out[pl.ds(y, 16, stride=16), :] = mine[y * 16:(y + 1) * 16]
    out_ref[rows, :] = own_out[...]
    copy.wait()


VM = pl.BlockSpec(memory_space=pltpu.VMEM)
SM = pl.BlockSpec(memory_space=pltpu.SMEM)
DMA = pltpu.SemaphoreType.DMA
LIMIT = 62 * 1024 * 1024


def vmem(*shape):
    return pltpu.VMEM(shape, f32)


SCRATCH = dict(
    ids=pltpu.VMEM((32, 16, 128), jnp.int32), classes=pltpu.VMEM((32, 16, 128), jnp.int32), cond=vmem(32, 16, 128),
    first=pltpu.VMEM((2, 256, 256), bf16), forward=pltpu.VMEM((2, 256, 256), bf16), cosine=pltpu.VMEM((2, 256, 256), bf16),
    eigen_x=vmem(256, 128), eigen_y=vmem(16, 256), eigen_z=vmem(16, 256), in_sem=DMA((9,)),
    field=vmem(2, 32, 16, 128), rows=vmem(2, 2, 32, 128), ext=vmem(2, 50, YE, 256), row_ext=vmem(2, 2, 16, 256),
    halo_send=DMA((40,)), halo_recv=DMA((40,)),
    root=vmem(2, XE, 48, 128), gain=vmem(2, XE, YE, 128), keep=vmem(2, XE, YE, 128),
    wa=vmem(3, 2, XE, 48, 128), wb=vmem(3, 2, XE, 48, 128), row_w=vmem(2, 2, 4, 16, 128), div=vmem(2, 256, 128), mixed=vmem(256, 256),
    s1=vmem(2, 256, 128), r2=vmem(2, 256, 128), s2=vmem(2, 256, 128), r3=vmem(2, 256, 128), s3=vmem(2, 256, 128),
    r4=vmem(2, 256, 128), s4=vmem(2, 256, 128), r5=vmem(2, 256, 128), lines=vmem(256, 256),
    own_out=vmem(256, 128), peer_out=vmem(256, 128),
    send_sem=DMA((4, 16)), recv_sem=DMA((4, 16)), last_send=DMA(()), last_recv=DMA(()),
)


def whole_kernel(ids_in, class_in, cond_in, first_in, forward_in, cosine_in, eigen_x_in, eigen_y_in, eigen_z_in, table_ref, normals_ref, out_ref, *scratch):
    s = dict(zip(SCRATCH, scratch))
    loads = [pltpu.make_async_copy(src, dst, s["in_sem"].at[k]) for k, (src, dst) in enumerate([
        (ids_in, s["ids"]), (class_in, s["classes"]), (cond_in, s["cond"]), (first_in, s["first"]), (forward_in, s["forward"]), (cosine_in, s["cosine"]),
        (eigen_x_in, s["eigen_x"]), (eigen_y_in, s["eigen_y"]), (eigen_z_in, s["eigen_z"])])]
    barrier = pltpu.get_barrier_semaphore()
    for load in loads[:3]:
        load.start()
    count = greet_groups(barrier) + greet_halo(barrier)
    for load in loads[3:]:
        load.start()
    for load in loads[:3]:
        load.wait()
    fill_field(s["ids"], s["classes"], s["cond"], table_ref, s["field"], s["rows"])
    pl.semaphore_wait(barrier, count)
    copies = halo_copies(s["field"], s["rows"], s["ext"], s["row_ext"], s["halo_send"], s["halo_recv"])
    for first, _ in INNER:
        start_all(copies, ("face", first))
    start_all(copies, "own", ("block",), ("row",), ("edge",))
    for load in loads[3:]:
        load.wait()
    heat_part(normals_ref, copies, s["ext"], s["row_ext"], s["first"], s["s1"], s["root"], s["gain"], s["keep"], s["wa"], s["wb"], s["row_w"], s["div"], s["mixed"])
    solve_part(s["s1"], s["forward"], s["cosine"], s["eigen_x"], s["eigen_y"], s["eigen_z"], out_ref, s["r2"], s["s2"], s["r3"], s["s3"],
               s["r4"], s["s4"], s["r5"], s["lines"], s["own_out"], s["peer_out"], s["mixed"],
               s["send_sem"], s["recv_sem"], s["last_send"], s["last_recv"])


def per_device(surface_ids, class_map, conductivity, normals, class_table):
    cosine = cosine_table()
    eigen = eigen_values()
    cosine_pair, forward_pair = jnp.asarray(halves(cosine)), jnp.asarray(halves(cosine.T.copy()))
    along_z = np.concatenate([np.arange(0, N, 2), np.arange(1, N, 2)])
    first_pair = jnp.asarray(halves(cosine.T[along_z].copy()))
    eigen_x = jnp.asarray(np.repeat(eigen[:, None], 128, axis=1))
    eigen_y = jnp.asarray(np.repeat(eigen.reshape(16, 16), 16, axis=1))
    eigen_z = jnp.asarray(np.tile(eigen.reshape(16, 16), (1, 16)))
    out = pl.pallas_call(
        whole_kernel,
        out_shape=jax.ShapeDtypeStruct((512, 128), f32),
        in_specs=[pl.BlockSpec(memory_space=pltpu.HBM)] * 9 + [SM, VM], out_specs=VM,
        scratch_shapes=list(SCRATCH.values()),
        compiler_params=pltpu.CompilerParams(collective_id=0, has_side_effects=True, vmem_limit_bytes=LIMIT),
    )(surface_ids, class_map, conductivity, first_pair, forward_pair, cosine_pair, eigen_x, eigen_y, eigen_z, class_table, normals)
    return out.reshape(32, 16, 128)


def solution(mesh):
    spec = P("gx", "gy", "gz")
    return jax.shard_map(
        per_device, mesh=mesh, in_specs=(spec, spec, spec, P(), P()), out_specs=spec, check_vma=False
    )
```
